32 devices in a mesh: var: 2 (over y), gx: 4 (over z), gy: 2 (over x), nd: 2 (over core).
Axes of the slice: x: 2, y: 2, z: 4, core: 2. Of those that a mesh axis runs over, the one named last changes fastest.
Arguments:
- right_side: float32 [8192, 256], P(('var', 'gx', 'gy', 'nd')), parts along dimension 0, may hold values from -8 to 8
- node_diag: float32 [8192], P(('var', 'gx', 'gy', 'nd')), parts along dimension 0, may hold values from 1 to 10
- local_coup: float32 [64, 7, 128, 128], P(('var', 'gx', 'gy', 'nd')), parts along dimension 0, may hold values from -0.01 to 0.01
- block_cols: int32 [32, 7], P(('gx', 'gy', 'nd')), may hold values from 0 to 3
- border_coup: float32 [32, 8, 128, 128], P(('var', 'gx', 'gy', 'nd')), parts along dimension 0, may hold values from -0.01 to 0.01
- border_send: int32 [16, 8], P(('gx', 'gy', 'nd')), may hold values from 0 to 1
- border_rows: int32 [16, 8], P(('gx', 'gy', 'nd')), may hold values from 0 to 1
Outputs:
- solution_field: float32 [8192, 256], P(('var', 'gx', 'gy', 'nd')), parts along dimension 0
The draws below stay inside these ranges and needn't reach their ends.
There are 2 independent parts, one for each index of `var`. The reference program is written for one: setup_inputs(seed, part) draws one part's arguments, and reference() takes and returns one part's arrays. A program takes and returns all parts, laid end to end along the dimension named above; an argument that names none is the same for every part. Nothing has to cross between parts.
Inputs may be any that keep to these rules, and one draw needn't show every extreme that they name: `block_cols`: block numbers within a patch. `border_send`: block numbers within the sending device. `border_rows`: block numbers within the receiving device.
All inputs are finite; a program needn't handle non-finite values.
Results may differ from the reference program's by a relative error of at most 0.0003.
Values sent between devices are 32-bit elements; how exact they have to be, the bound alone decides.
A program may use at most 64 MiB of HBM per device.

```python
import math
import jax
import jax.numpy as jnp
from jax import lax

BS = 128
COLS = 256
NB = 2
NNZ = 7
BB = 2
ITERS = 2
DEVS = 16
PATCH = 4
NBLK = 32
NODES = 4096
N_GX = 4
N_GY = 2
N_ND = 2


def set_ends(drawn, stream_key, low, high):
    longest = drawn.shape.index(max(drawn.shape))
    spots = []
    for shift in (0, 1):
        where = [jax.random.randint(jax.random.fold_in(stream_key, axis), (), 0, length) for axis, length in enumerate(drawn.shape)]
        where[longest] = (where[longest] + shift) % drawn.shape[longest]
        spots.append(tuple(where))
    return drawn.at[spots[0]].set(low).at[spots[1]].set(high)


def block_levels(stream_key, shape, split, low, high):
    def one(axis_at, blocks):
        draws = jax.random.uniform(jax.random.fold_in(jax.random.fold_in(stream_key, 6), axis_at), (blocks,), jnp.float32, low / len(split), high / len(split))
        return jnp.repeat(jnp.exp(draws), shape[axis_at] // blocks).reshape((-1,) + (1,) * (len(shape) - axis_at - 1))

    level = one(*split[0])
    for cut in split[1:]:
        level = level * one(*cut)
    return level


def centred(rng, dims, spread, limit, shards=(), kind=jnp.bfloat16):
    drawn = jax.random.normal(rng, dims, jnp.float32) * spread
    if len(shards) > 0:
        drawn = block_levels(rng, dims, shards, -0.22, 0.18) * drawn
    return jnp.clip(drawn, min=-limit, max=limit).astype(kind)


def setup_inputs(seed: int = 0, part: int = 0) -> dict:
    splits = jax.random.split(jax.random.key(seed), 8)
    part_keys = jax.random.split(jax.random.fold_in(splits[7], part), 8)
    return {
        "right_side": centred(part_keys[0], (NODES, COLS), 1.0, 8.0, ((0, 16),), jnp.float32),
        "node_diag": jnp.clip(jnp.exp(math.log(10.0) - 2.3025851 * jax.random.uniform(part_keys[1], (NODES,), jnp.float32) ** block_levels(part_keys[1], (NODES,), ((0, 16),), -0.2, 0.2)), 1.0, 10.0),
        "local_coup": jnp.clip(jax.random.uniform(part_keys[2], (NBLK, NNZ, BS, BS), jnp.float32, -0.01, 0.01) * block_levels(part_keys[2], (NBLK, NNZ, BS, BS), ((0, 16),), -0.4, 0.0), -0.01, 0.01),
        "block_cols": set_ends(jax.random.randint(splits[3], (NBLK, NNZ), 0, PATCH), jax.random.fold_in(splits[3], 1), 0, PATCH - 1).astype(jnp.int32),
        "border_coup": jnp.clip(jax.random.uniform(part_keys[4], (DEVS, 4 * BB, BS, BS), jnp.float32, -0.01, 0.01) * block_levels(part_keys[4], (DEVS, 4 * BB, BS, BS), ((0, 16),), -0.4, 0.0), -0.01, 0.01),
        "border_send": set_ends(jax.random.randint(splits[5], (DEVS, 4 * BB), 0, NB), jax.random.fold_in(splits[5], 1), 0, NB - 1).astype(jnp.int32),
        "border_rows": set_ends(jax.random.randint(splits[6], (DEVS, 4 * BB), 0, NB), jax.random.fold_in(splits[6], 1), 0, NB - 1).astype(jnp.int32),
    }


def apply_prec(field, node_diag, local_coup, block_cols, border_coup, border_send, border_rows):
    blocks = field.reshape(NBLK, BS, COLS)
    diag_blocks = node_diag.reshape(NBLK, BS)
    hp = lax.Precision.HIGHEST

    def one_device(dev):
        gxi = dev // (N_GY * N_ND)
        gyi = (dev // N_ND) % N_GY
        ndi = dev % N_ND
        pstart = (dev // N_ND) * PATCH
        patch = lax.dynamic_slice_in_dim(blocks, pstart, PATCH, 0)
        picks = lax.dynamic_slice_in_dim(block_cols, dev * NB, NB, 0)
        coup = lax.dynamic_slice_in_dim(local_coup, dev * NB, NB, 0)
        own = lax.dynamic_slice_in_dim(blocks, dev * NB, NB, 0)
        diag = lax.dynamic_slice_in_dim(diag_blocks, dev * NB, NB, 0)
        picked = jnp.take(patch, picks, axis=0)
        result = diag[:, :, None] * own + jnp.einsum("bkij,bkjc->bic", coup, picked, precision=hp)
        pcoup = lax.dynamic_slice_in_dim(local_coup, pstart, PATCH, 0)
        pcols = lax.dynamic_slice_in_dim(block_cols, pstart, PATCH, 0)
        tterms = jnp.einsum("pkji,pjc->pkic", pcoup, patch, precision=hp).reshape(PATCH * NNZ, BS, COLS)
        mine = ndi * NB + jnp.arange(NB, dtype=jnp.int32)
        tonehot = (pcols.reshape(PATCH * NNZ)[None, :] == mine[:, None]).astype(field.dtype)
        result = result + jnp.einsum("nq,qic->nic", tonehot, tterms, precision=hp)
        left = (((gxi - 1) % N_GX) * N_GY + gyi) * N_ND + ndi
        right = (((gxi + 1) % N_GX) * N_GY + gyi) * N_ND + ndi
        down = (gxi * N_GY + jnp.maximum(gyi - 1, 0)) * N_ND + ndi
        upper = (gxi * N_GY + jnp.minimum(gyi + 1, N_GY - 1)) * N_ND + ndi
        lowok = (gyi > 0).astype(field.dtype)
        highok = (gyi < N_GY - 1).astype(field.dtype)
        valids = [1.0, 1.0, lowok, highok]
        parts = []
        for turn, sender in enumerate([left, right, down, upper]):
            slots = jnp.take(border_send, sender, axis=0)[turn * BB:(turn + 1) * BB]
            index = sender * NB + slots
            parts.append(jnp.take(blocks, index, axis=0) * valids[turn])
        received = jnp.concatenate(parts, axis=0)
        bcoup = jnp.take(border_coup, dev, axis=0)
        contrib = jnp.einsum("mij,mjc->mic", bcoup, received, precision=hp)
        targets = jnp.take(border_rows, dev, axis=0)
        onehot = (targets[None, :] == jnp.arange(NB, dtype=jnp.int32)[:, None]).astype(field.dtype)
        result = result + jnp.einsum("nm,mic->nic", onehot, contrib, precision=hp)
        backs = []
        back_valids = [1.0, 1.0, highok, lowok]
        for turn, source in enumerate([right, left, upper, down]):
            qcoup = jnp.take(border_coup, source, axis=0)[turn * BB:(turn + 1) * BB]
            qrows = jnp.take(border_rows, source, axis=0)[turn * BB:(turn + 1) * BB]
            qblocks = jnp.take(blocks, source * NB + qrows, axis=0)
            backs.append(jnp.einsum("mji,mjc->mic", qcoup, qblocks, precision=hp) * back_valids[turn])
        returned = jnp.concatenate(backs, axis=0)
        sendto = jnp.take(border_send, dev, axis=0)
        sonehot = (sendto[None, :] == jnp.arange(NB, dtype=jnp.int32)[:, None]).astype(field.dtype)
        return result + jnp.einsum("nm,mic->nic", sonehot, returned, precision=hp)

    out = lax.map(one_device, jnp.arange(DEVS, dtype=jnp.int32))
    return out.reshape(NODES, COLS)


def reference(right_side, node_diag, local_coup, block_cols, border_coup, border_send, border_rows):
    solution_field = jnp.zeros_like(right_side)
    residual = right_side
    direction = right_side
    norm_now = jnp.sum(residual * residual, axis=0)
    for step in range(ITERS):
        image = apply_prec(direction, node_diag, local_coup, block_cols, border_coup, border_send, border_rows)
        alpha = norm_now / jnp.sum(direction * image, axis=0)
        solution_field = solution_field + alpha * direction
        residual = residual - alpha * image
        norm_next = jnp.sum(residual * residual, axis=0)
        direction = residual + (norm_next / norm_now) * direction
        norm_now = norm_next
    return solution_field
```

```python
import functools

import jax
import jax.numpy as jnp
from jax import lax
from jax.experimental import pallas as pl
from jax.experimental.pallas import tpu as pltpu
from jax.sharding import PartitionSpec as P

HP = lax.Precision.HIGHEST
LEFT, RIGHT, DOWN, UP = range(4)
OPPOSITE = (RIGHT, LEFT, UP, DOWN)


def mm(a, b):
    return jnp.dot(a, b, precision=HP, preferred_element_type=jnp.float32)


def kernel(
    sizes,
    rhs, diag, local, cols, border, send, rows,
    out,
    fields, images, local_v, border_v, border_in, pair_out, pair_in, marks, marks_in,
    prec, acc, sums,
    load_sem, f_send, f_recv, m_send, m_recv, k_send, k_recv, p_send, p_recv,
    w_send, w_recv, s_send, s_recv,
):
    nx, ny, nn = sizes
    total = nx * ny * nn
    nb, nnz, bs, _ = local_v.shape
    per = border_v.shape[0] // 4
    size, width = out.shape
    gx, gy, nd = lax.axis_index("gx"), lax.axis_index("gy"), lax.axis_index("nd")
    me = (gx * ny + gy) * nn + nd
    low = gy > 0
    high = gy < ny - 1
    targets = (
        {"gx": lax.rem(gx + nx - 1, nx)},
        {"gx": lax.rem(gx + 1, nx)},
        {"gy": jnp.maximum(gy - 1, 0)},
        {"gy": jnp.minimum(gy + 1, ny - 1)},
    )
    partner = {"nd": 1 - nd}

    def peer(step):
        other = lax.rem(me + step, total)
        return {"gx": other // (ny * nn), "gy": lax.rem(other // nn, ny), "nd": lax.rem(other, nn)}

    def over_peers(body):
        if total <= 16:
            for step in range(1, total):
                body(step)
        else:
            lax.fori_loop(1, total, lambda step, _: (body(step), 0)[1], 0)

    def side(turn, body):
        if turn == DOWN:
            pl.when(low)(body)
        elif turn == UP:
            pl.when(high)(body)
        else:
            body()

    def remote(src, dst, ssem, rsem, where):
        return pltpu.make_async_remote_copy(
            src_ref=src, dst_ref=dst, send_sem=ssem, recv_sem=rsem,
            device_id=where, device_id_type=pl.DeviceIdType.MESH,
        )

    loads = [
        pltpu.make_async_copy(local, local_v, load_sem.at[0]),
        pltpu.make_async_copy(rhs, fields.at[0], load_sem.at[1]),
        pltpu.make_async_copy(border.at[0], border_v, load_sem.at[2]),
    ]
    for load in loads:
        load.start()

    barrier = pltpu.get_barrier_semaphore()
    over_peers(
        lambda step: pl.semaphore_signal(
            barrier, inc=1, device_id=peer(step), device_id_type=pl.DeviceIdType.MESH
        )
    )
    for m in range(4 * per):
        marks[m : m + 1, :] = jnp.full((1, 128), send[0, m], jnp.int32).astype(jnp.float32)
        at = 4 * per + m
        marks[at : at + 1, :] = jnp.full((1, 128), rows[0, m], jnp.int32).astype(jnp.float32)
    pl.semaphore_wait(barrier, total - 1)

    def mark_copy(turn):
        opp = OPPOSITE[turn]
        return remote(marks, marks_in.at[opp], k_send.at[turn], k_recv.at[opp], targets[turn])

    def border_copy(turn):
        opp = OPPOSITE[turn]
        return remote(
            border.at[0, pl.ds(turn * per, per)], border_in.at[opp],
            m_send.at[turn], m_recv.at[opp], targets[turn],
        )

    def field_copy(turn):
        opp = OPPOSITE[turn]
        return remote(rhs, fields.at[2 + opp], f_send.at[turn], f_recv.at[opp], targets[turn])

    for make in (mark_copy, border_copy, field_copy):
        for turn in range(4):
            side(turn, lambda: make(turn).start())
    field_pair = remote(rhs, fields.at[1], f_send.at[4], f_recv.at[4], partner)
    field_pair.start()

    loads[0].wait()
    for i in range(nb):
        for j in range(nb):
            own = jnp.zeros((bs, bs), jnp.float32)
            far = jnp.zeros((bs, bs), jnp.float32)
            for k in range(nnz):
                block = local_v[i, k]
                col = cols[i, k]
                own = own + jnp.where(col == nd * nb + j, 1.0, 0.0) * block
                far = far + jnp.where(col == (1 - nd) * nb + j, 1.0, 0.0) * block
            prec[0, i * bs : (i + 1) * bs, j * bs : (j + 1) * bs] = own
            pair_out[i * bs : (i + 1) * bs, j * bs : (j + 1) * bs] = far
    pair = remote(pair_out, pair_in, p_send, p_recv, partner)
    pair.start()
    prec[0] = prec[0] + prec[0].T

    eye = lax.broadcasted_iota(jnp.int32, (size, size), 0) == lax.broadcasted_iota(
        jnp.int32, (size, size), 1
    )
    column = jnp.sum(
        jnp.where(eye, jnp.broadcast_to(diag[...], (size, size)), 0.0), axis=1, keepdims=True
    )

    loads[1].wait()
    acc[...] = column * fields[0] + mm(prec[0], fields[0])
    pair.wait()
    prec[1] = pair_out[...] + pair_in[...].T
    field_pair.wait()
    acc[...] += mm(prec[1], fields[1])

    loads[2].wait()

    def couple(turn):
        opp = OPPOSITE[turn]
        mark_copy(turn).wait_send()
        border_copy(turn).wait_send()
        remote(marks, marks_in.at[turn], k_send.at[turn], k_recv.at[turn], targets[turn]).wait_recv()
        remote(
            border.at[0, pl.ds(turn * per, per)], border_in.at[turn],
            m_send.at[turn], m_recv.at[turn], targets[turn],
        ).wait_recv()
        back = [border_in[turn, s].T for s in range(per)]
        for i in range(nb):
            for j in range(nb):
                block = jnp.zeros((bs, bs), jnp.float32)
                for s in range(per):
                    m, n = turn * per + s, opp * per + s
                    to = jnp.where(rows[0, m] == i, 1.0, 0.0)
                    took = jnp.where(marks_in[turn, m : m + 1, :] == float(j), 1.0, 0.0)
                    block = block + (to * took) * border_v[m]
                    to = jnp.where(send[0, n] == i, 1.0, 0.0)
                    at = 4 * per + n
                    took = jnp.where(marks_in[turn, at : at + 1, :] == float(j), 1.0, 0.0)
                    block = block + (to * took) * back[s]
                prec[2 + turn, i * bs : (i + 1) * bs, j * bs : (j + 1) * bs] = block

    def join(turn):
        field_copy(turn).wait_send()
        remote(
            rhs, fields.at[2 + turn], f_send.at[turn], f_recv.at[turn], targets[turn]
        ).wait_recv()
        acc[...] += mm(prec[2 + turn], fields[2 + turn])

    for turn in (DOWN, UP, LEFT, RIGHT):
        side(turn, lambda: couple(turn))
    for turn in (DOWN, UP, LEFT, RIGHT):
        side(turn, lambda: join(turn))

    images[0] = acc[...]

    def image_copy(turn, slot):
        where = partner if turn is None else targets[turn]
        return remote(images.at[0], images.at[slot], w_send.at[slot - 1], w_recv.at[slot - 1], where)

    image_copy(RIGHT, 2).start()
    side(UP, lambda: image_copy(UP, 3).start())
    image_copy(None, 1).start()

    def share(phase, first, second):
        sums[phase, me, 0:1, :] = first
        sums[phase, me, 1:2, :] = second
        over_peers(
            lambda step: remote(
                sums.at[phase, me], sums.at[phase, me], s_send.at[phase], s_recv.at[phase],
                peer(step),
            ).start()
        )

    def collect(phase):
        every = sums.at[phase, pl.ds(0, total - 1)]
        done = remote(every, every, s_send.at[phase], s_recv.at[phase], partner)
        done.wait_send()
        done.wait_recv()
        both = jnp.sum(sums[phase], axis=0)
        return both[0:1, :], both[1:2, :]

    def column_sum(a):
        return jnp.sum(a, axis=0, keepdims=True)

    share(0, column_sum(fields[0] * fields[0]), column_sum(fields[0] * images[0]))
    norm, curve = collect(0)
    alpha = norm / curve

    acc[...] = fields[0] - alpha * images[0]
    image_copy(None, 1).wait()
    far = fields[1] - alpha * images[1]
    images[1] = column * acc[...] + mm(prec[0], acc[...]) + mm(prec[1], far)

    def add_below():
        image_copy(UP, 3).wait_recv()
        images[1] += 2.0 * mm(prec[2 + DOWN], fields[2 + DOWN] - alpha * images[3])

    side(DOWN, add_below)
    side(UP, lambda: image_copy(UP, 3).wait_send())
    image_copy(RIGHT, 2).wait()
    images[1] += 2.0 * mm(prec[2 + LEFT], fields[2 + LEFT] - alpha * images[2])
    share(1, column_sum(acc[...] * acc[...]), column_sum(acc[...] * images[1]))
    norm_next, quad = collect(1)
    ratio = norm_next / norm
    alpha_next = norm_next / (quad - ratio * norm_next / alpha)
    out[...] = alpha * fields[0] + alpha_next * (acc[...] + ratio * fields[0])


def shards(sizes, right_side, node_diag, local_coup, block_cols, border_coup, border_send, border_rows):
    size, width = right_side.shape
    nb, nnz, bs, _ = local_coup.shape
    slots = border_coup.shape[1]
    per = slots // 4
    total = sizes[0] * sizes[1] * sizes[2]
    vmem = pl.BlockSpec(memory_space=pltpu.VMEM)
    smem = pl.BlockSpec(memory_space=pltpu.SMEM)
    anywhere = pl.BlockSpec(memory_space=pl.ANY)
    f32 = jnp.float32
    dma = pltpu.SemaphoreType.DMA
    return pl.pallas_call(
        functools.partial(kernel, sizes),
        out_shape=jax.ShapeDtypeStruct((size, width), f32),
        in_specs=[anywhere, vmem, anywhere, smem, anywhere, smem, smem],
        out_specs=vmem,
        scratch_shapes=[
            pltpu.VMEM((6, size, width), f32),
            pltpu.VMEM((4, size, width), f32),
            pltpu.VMEM((nb, nnz, bs, bs), f32),
            pltpu.VMEM((slots, bs, bs), f32),
            pltpu.VMEM((4, per, bs, bs), f32),
            pltpu.VMEM((size, size), f32),
            pltpu.VMEM((size, size), f32),
            pltpu.VMEM((2 * slots, 128), f32),
            pltpu.VMEM((4, 2 * slots, 128), f32),
            pltpu.VMEM((6, size, size), f32),
            pltpu.VMEM((size, width), f32),
            pltpu.VMEM((2, total, 2, width), f32),
            dma((3,)), dma((5,)), dma((5,)), dma((4,)), dma((4,)), dma((4,)), dma((4,)),
            dma, dma, dma((3,)), dma((3,)), dma((2,)), dma((2,)),
        ],
        compiler_params=pltpu.CompilerParams(
            collective_id=0, has_side_effects=True, vmem_limit_bytes=40 * 1024 * 1024
        ),
    )(
        right_side, node_diag.reshape(1, size), local_coup, block_cols, border_coup,
        border_send, border_rows,
    )


def solution(mesh):
    in_specs = (
        P(("var", "gx", "gy", "nd"), None),
        P(("var", "gx", "gy", "nd")),
        P(("var", "gx", "gy", "nd"), None, None, None),
        P(("gx", "gy", "nd"), None),
        P(("var", "gx", "gy", "nd"), None, None, None),
        P(("gx", "gy", "nd"), None),
        P(("gx", "gy", "nd"), None),
    )
    out_specs = P(("var", "gx", "gy", "nd"), None)
    sizes = tuple(mesh.shape[axis] for axis in ("gx", "gy", "nd"))
    return jax.shard_map(
        functools.partial(shards, sizes), mesh=mesh, in_specs=in_specs, out_specs=out_specs,
        check_vma=False,
    )
```

```python
import functools

import jax
import jax.numpy as jnp
from jax import lax
from jax.experimental import pallas as pl
from jax.experimental.pallas import tpu as pltpu
from jax.sharding import PartitionSpec as P

HP = lax.Precision.HIGHEST
LEFT, RIGHT, DOWN, UP = range(4)
CHUNK = 128


def mm(a, b):
    return jnp.dot(a, b, precision=HP, preferred_element_type=jnp.float32)


def column_sum(a):
    return jnp.sum(a, axis=0, keepdims=True)


def kernel(
    sizes,
    rhs, diag_hbm, local, cols_hbm, border, send_hbm, rows_hbm,
    out,
    fields, images, prods_out, prods_in, local_v, border_v, border_in, pair_out, pair_in,
    marks, marks_in, prec, work, sums, diag, cols, send, rows,
    load_sem, f_send, f_recv, m_send, m_recv, k_send, k_recv, p_send, p_recv,
    b_send, b_recv, w_send, w_recv, s_send, s_recv,
):
    nx, ny, nn = sizes
    total = nx * ny * nn
    nb, nnz, bs, _ = local_v.shape
    per = border_v.shape[0] // 4
    size, width = out.shape
    chunks = width // CHUNK
    gx, gy, nd = lax.axis_index("gx"), lax.axis_index("gy"), lax.axis_index("nd")
    me = (gx * ny + gy) * nn + nd
    low = gy > 0
    high = gy < ny - 1
    left = {"gx": lax.rem(gx + nx - 1, nx)}
    right = {"gx": lax.rem(gx + 1, nx)}
    below = {"gy": jnp.maximum(gy - 1, 0)}
    above = {"gy": jnp.minimum(gy + 1, ny - 1)}
    partner = {"nd": 1 - nd}
    forward = (right, above)
    backward = (left, below)
    has_next = (None, high)
    has_last = (None, low)
    came = (LEFT, DOWN)
    goes = (RIGHT, UP)

    def given(condition, body):
        if condition is None:
            body()
        else:
            pl.when(condition)(body)

    def part(c):
        return pl.ds(c * CHUNK, CHUNK)

    def span(c):
        return slice(c * CHUNK, (c + 1) * CHUNK)

    def peer(step):
        other = lax.rem(me + step, total)
        return {"gx": other // (ny * nn), "gy": lax.rem(other // nn, ny), "nd": lax.rem(other, nn)}

    def over_peers(body):
        if total <= 16:
            for step in range(1, total):
                body(step)
        else:
            lax.fori_loop(1, total, lambda step, _: (body(step), 0)[1], 0)

    def remote(src, dst, ssem, rsem, where):
        return pltpu.make_async_remote_copy(
            src_ref=src, dst_ref=dst, send_sem=ssem, recv_sem=rsem,
            device_id=where, device_id_type=pl.DeviceIdType.MESH,
        )

    pairs = (
        (send_hbm, send), (rows_hbm, rows), (cols_hbm, cols), (local, local_v),
        (border.at[0], border_v), (rhs, fields.at[0]), (diag_hbm, diag),
    )
    loads = [pltpu.make_async_copy(src, dst, load_sem.at[i]) for i, (src, dst) in enumerate(pairs)]
    for load in loads:
        load.start()

    barrier = pltpu.get_barrier_semaphore()
    over_peers(
        lambda step: pl.semaphore_signal(
            barrier, inc=1, device_id=peer(step), device_id_type=pl.DeviceIdType.MESH
        )
    )
    loads[0].wait()
    loads[1].wait()
    for m in range(4 * per):
        marks[m : m + 1, :] = jnp.full((1, 128), send[0, m], jnp.int32).astype(jnp.float32)
        at = 4 * per + m
        marks[at : at + 1, :] = jnp.full((1, 128), rows[0, m], jnp.int32).astype(jnp.float32)
    pl.semaphore_wait(barrier, total - 1)

    mark_copy = [
        remote(marks, marks_in.at[a], k_send.at[a], k_recv.at[a], forward[a]) for a in range(2)
    ]
    border_copy = [
        remote(
            border.at[0, pl.ds(goes[a] * per, per)], border_in.at[a],
            m_send.at[a], m_recv.at[a], forward[a],
        )
        for a in range(2)
    ]
    field_copy = [
        [
            remote(
                rhs.at[:, part(c)], fields.at[2 + a, :, part(c)],
                f_send.at[a, c], f_recv.at[a, c], forward[a],
            )
            for c in range(chunks)
        ]
        for a in range(2)
    ]
    back_copy = [
        [
            remote(
                prods_out.at[a, :, part(c)], prods_in.at[a, :, part(c)],
                b_send.at[a, c], b_recv.at[a, c], backward[a],
            )
            for c in range(chunks)
        ]
        for a in range(2)
    ]
    image_copy = [
        [
            remote(
                images.at[0, :, part(c)], images.at[slot, :, part(c)],
                w_send.at[i, c], w_recv.at[i, c], where,
            )
            for c in range(chunks)
        ]
        for i, (slot, where) in enumerate(((2, right), (3, above), (1, partner)))
    ]
    field_pair = remote(rhs, fields.at[1], f_send.at[2, 0], f_recv.at[2, 0], partner)
    pair = remote(pair_out, pair_in, p_send, p_recv, partner)

    for a in range(2):
        given(has_next[a], lambda: mark_copy[a].start())
    for a in range(2):
        given(has_next[a], lambda: border_copy[a].start())
    for c in range(chunks):
        for a in range(2):
            given(has_next[a], lambda: field_copy[a][c].start())
    field_pair.start()

    loads[2].wait()
    loads[3].wait()
    for i in range(nb):
        for j in range(nb):
            own = jnp.zeros((bs, bs), jnp.float32)
            far = jnp.zeros((bs, bs), jnp.float32)
            for k in range(nnz):
                block = local_v[i, k]
                col = cols[i, k]
                own = own + jnp.where(col == nd * nb + j, 1.0, 0.0) * block
                far = far + jnp.where(col == (1 - nd) * nb + j, 1.0, 0.0) * block
            prec[0, i * bs : (i + 1) * bs, j * bs : (j + 1) * bs] = own
            pair_out[i * bs : (i + 1) * bs, j * bs : (j + 1) * bs] = far
    pair.start()
    prec[0] = prec[0] + prec[0].T

    loads[4].wait()
    loads[5].wait()

    def couple(a):
        mark_copy[a].wait_recv()
        border_copy[a].wait_recv()
        turn, opp = came[a], goes[a]
        back = [border_in[a, s].T for s in range(per)]
        for i in range(nb):
            for j in range(nb):
                block = jnp.zeros((bs, bs), jnp.float32)
                for s in range(per):
                    m, n = turn * per + s, opp * per + s
                    to = jnp.where(rows[0, m] == i, 1.0, 0.0)
                    took = jnp.where(marks_in[a, m : m + 1, :] == float(j), 1.0, 0.0)
                    block = block + (to * took) * border_v[m]
                    to = jnp.where(send[0, n] == i, 1.0, 0.0)
                    at = 4 * per + n
                    took = jnp.where(marks_in[a, at : at + 1, :] == float(j), 1.0, 0.0)
                    block = block + (to * took) * back[s]
                prec[2 + a, i * bs : (i + 1) * bs, j * bs : (j + 1) * bs] = block
        prec[4 + a] = prec[2 + a].T
        for c in range(chunks):
            prods_out[a, :, span(c)] = mm(prec[4 + a], fields[0, :, span(c)])
            back_copy[a][c].start()

    given(has_last[1], lambda: couple(1))
    given(has_last[0], lambda: couple(0))

    loads[6].wait()
    eye = lax.broadcasted_iota(jnp.int32, (size, size), 0) == lax.broadcasted_iota(
        jnp.int32, (size, size), 1
    )
    column = jnp.sum(
        jnp.where(eye, jnp.broadcast_to(diag[...], (size, size)), 0.0), axis=1, keepdims=True
    )
    work[...] = column * fields[0] + mm(prec[0], fields[0])
    pair.wait()
    prec[1] = pair_out[...] + pair_in[...].T
    field_pair.wait()
    work[...] += mm(prec[1], fields[1])

    for c in range(chunks):

        def from_last(a):
            field_copy[a][c].wait_recv()
            work[:, span(c)] += mm(prec[2 + a], fields[2 + a, :, span(c)])

        def from_next(a):
            back_copy[a][c].wait_recv()
            work[:, span(c)] += prods_in[a, :, span(c)]

        for a in (1, 0):
            given(has_last[a], lambda: from_last(a))
            given(has_next[a], lambda: from_next(a))
        images[0, :, span(c)] = work[:, span(c)]
        image_copy[0][c].start()
        given(high, lambda: image_copy[1][c].start())
        image_copy[2][c].start()

    def share(phase, first, second):
        sums[phase, me, 0:1, :] = first
        sums[phase, me, 1:2, :] = second
        over_peers(
            lambda step: remote(
                sums.at[phase, me], sums.at[phase, me], s_send.at[phase], s_recv.at[phase],
                peer(step),
            ).start()
        )

    def collect(phase):
        every = sums.at[phase, pl.ds(0, total - 1)]
        done = remote(every, every, s_send.at[phase], s_recv.at[phase], partner)
        done.wait_send()
        done.wait_recv()
        both = jnp.sum(sums[phase], axis=0)
        return both[0:1, :], both[1:2, :]

    share(0, column_sum(fields[0] * fields[0]), column_sum(fields[0] * images[0]))
    norm, curve = collect(0)
    alpha = norm / curve

    out[...] = fields[0] - alpha * images[0]
    work[...] = column * out[...] + mm(prec[0], out[...])
    for c in range(chunks):

        def quad_last(a):
            image_copy[a][c].wait_recv()
            behind = fields[2 + a, :, span(c)] - alpha[:, span(c)] * images[2 + a, :, span(c)]
            work[:, span(c)] += 2.0 * mm(prec[2 + a], behind)

        image_copy[2][c].wait_recv()
        across = fields[1, :, span(c)] - alpha[:, span(c)] * images[1, :, span(c)]
        work[:, span(c)] += mm(prec[1], across)
        for a in (1, 0):
            given(has_last[a], lambda: quad_last(a))
    share(1, column_sum(out[...] * out[...]), column_sum(out[...] * work[...]))

    for a in range(2):
        given(has_next[a], lambda: mark_copy[a].wait_send())
        given(has_next[a], lambda: border_copy[a].wait_send())
        for c in range(chunks):
            given(has_next[a], lambda: field_copy[a][c].wait_send())
            given(has_last[a], lambda: back_copy[a][c].wait_send())
            given(has_next[a], lambda: image_copy[a][c].wait_send())
    for c in range(chunks):
        image_copy[2][c].wait_send()

    norm_next, quad = collect(1)
    ratio = norm_next / norm
    alpha_next = norm_next / (quad - ratio * norm_next / alpha)
    out[...] = (alpha + alpha_next * ratio) * fields[0] + alpha_next * out[...]


def shards(sizes, right_side, node_diag, local_coup, block_cols, border_coup, border_send, border_rows):
    size, width = right_side.shape
    nb, nnz, bs, _ = local_coup.shape
    slots = border_coup.shape[1]
    per = slots // 4
    total = sizes[0] * sizes[1] * sizes[2]
    chunks = width // CHUNK
    hbm = pl.BlockSpec(memory_space=pltpu.HBM)
    f32 = jnp.float32
    dma = pltpu.SemaphoreType.DMA
    return pl.pallas_call(
        functools.partial(kernel, sizes),
        out_shape=jax.ShapeDtypeStruct((size, width), f32),
        in_specs=[hbm] * 7,
        out_specs=pl.BlockSpec(memory_space=pltpu.VMEM),
        scratch_shapes=[
            pltpu.VMEM((4, size, width), f32),
            pltpu.VMEM((4, size, width), f32),
            pltpu.VMEM((2, size, width), f32),
            pltpu.VMEM((2, size, width), f32),
            pltpu.VMEM((nb, nnz, bs, bs), f32),
            pltpu.VMEM((slots, bs, bs), f32),
            pltpu.VMEM((2, per, bs, bs), f32),
            pltpu.VMEM((size, size), f32),
            pltpu.VMEM((size, size), f32),
            pltpu.VMEM((2 * slots, 128), f32),
            pltpu.VMEM((2, 2 * slots, 128), f32),
            pltpu.VMEM((6, size, size), f32),
            pltpu.VMEM((size, width), f32),
            pltpu.VMEM((2, total, 2, width), f32),
            pltpu.VMEM((1, size), f32),
            pltpu.SMEM((nb, nnz), jnp.int32),
            pltpu.SMEM((1, slots), jnp.int32),
            pltpu.SMEM((1, slots), jnp.int32),
            dma((7,)), dma((3, chunks)), dma((3, chunks)), dma((2,)), dma((2,)), dma((2,)), dma((2,)),
            dma, dma, dma((2, chunks)), dma((2, chunks)), dma((3, chunks)), dma((3, chunks)),
            dma((2,)), dma((2,)),
        ],
        compiler_params=pltpu.CompilerParams(
            collective_id=0, has_side_effects=True, vmem_limit_bytes=48 * 1024 * 1024
        ),
    )(
        right_side, node_diag.reshape(1, size), local_coup, block_cols, border_coup,
        border_send, border_rows,
    )


def solution(mesh):
    in_specs = (
        P(("var", "gx", "gy", "nd"), None),
        P(("var", "gx", "gy", "nd")),
        P(("var", "gx", "gy", "nd"), None, None, None),
        P(("gx", "gy", "nd"), None),
        P(("var", "gx", "gy", "nd"), None, None, None),
        P(("gx", "gy", "nd"), None),
        P(("gx", "gy", "nd"), None),
    )
    out_specs = P(("var", "gx", "gy", "nd"), None)
    sizes = tuple(mesh.shape[axis] for axis in ("gx", "gy", "nd"))
    return jax.shard_map(
        functools.partial(shards, sizes), mesh=mesh, in_specs=in_specs, out_specs=out_specs,
        check_vma=False,
    )
```

```python
import functools

import jax
import jax.numpy as jnp
from jax import lax
from jax.experimental import pallas as pl
from jax.experimental.pallas import tpu as pltpu
from jax.sharding import PartitionSpec as P

LEFT, RIGHT, DOWN, UP = range(4)
CHUNK = 128


def halves(a):
    high = a.astype(jnp.bfloat16)
    return high, (a - high.astype(jnp.float32)).astype(jnp.bfloat16)


def dot(a, b):
    return jnp.dot(a, b, preferred_element_type=jnp.float32)


def mm(a, b):
    a_high, a_low = halves(a)
    b_high, b_low = halves(b)
    return dot(a_high, b_high) + (dot(a_high, b_low) + dot(a_low, b_high))


def column_sum(a):
    return jnp.sum(a, axis=0, keepdims=True)


def kernel(
    sizes,
    rhs, diag_hbm, local, cols_hbm, border, send_hbm, rows_hbm,
    out,
    fields, images, prods_out, prods_in, local_v, border_v, border_in, pair_out, pair_in,
    marks, marks_in, prec, turned, work, sums, diag, cols, send, rows,
    load_sem, f_send, f_recv, m_send, m_recv, k_send, k_recv, p_send, p_recv,
    b_send, b_recv, w_send, w_recv, s_send, s_recv,
):
    nx, ny, nn = sizes
    total = nx * ny * nn
    nb, nnz, bs, _ = local_v.shape
    per = border_v.shape[0] // 4
    size, width = out.shape
    chunks = width // CHUNK
    gx, gy, nd = lax.axis_index("gx"), lax.axis_index("gy"), lax.axis_index("nd")
    me = (gx * ny + gy) * nn + nd
    low = gy > 0
    high = gy < ny - 1
    left = {"gx": lax.rem(gx + nx - 1, nx)}
    right = {"gx": lax.rem(gx + 1, nx)}
    below = {"gy": jnp.maximum(gy - 1, 0)}
    above = {"gy": jnp.minimum(gy + 1, ny - 1)}
    partner = {"nd": 1 - nd}
    forward = (right, above)
    backward = (left, below)
    has_next = (None, high)
    has_last = (None, low)
    came = (LEFT, DOWN)
    goes = (RIGHT, UP)

    def given(condition, body):
        if condition is None:
            body()
        else:
            pl.when(condition)(body)

    def part(c):
        return pl.ds(c * CHUNK, CHUNK)

    def span(c):
        return slice(c * CHUNK, (c + 1) * CHUNK)

    def peer(step):
        other = lax.rem(me + step, total)
        return {"gx": other // (ny * nn), "gy": lax.rem(other // nn, ny), "nd": lax.rem(other, nn)}

    def over_peers(body):
        if total <= 16:
            for step in range(1, total):
                body(step)
        else:
            lax.fori_loop(1, total, lambda step, _: (body(step), 0)[1], 0)

    def remote(src, dst, ssem, rsem, where):
        return pltpu.make_async_remote_copy(
            src_ref=src, dst_ref=dst, send_sem=ssem, recv_sem=rsem,
            device_id=where, device_id_type=pl.DeviceIdType.MESH,
        )

    pairs = (
        (send_hbm, send), (rows_hbm, rows), (cols_hbm, cols), (local, local_v),
        (border.at[0], border_v), (rhs, fields.at[0]), (diag_hbm, diag),
    )
    loads = [pltpu.make_async_copy(src, dst, load_sem.at[i]) for i, (src, dst) in enumerate(pairs)]
    for load in loads:
        load.start()

    barrier = pltpu.get_barrier_semaphore()
    over_peers(
        lambda step: pl.semaphore_signal(
            barrier, inc=1, device_id=peer(step), device_id_type=pl.DeviceIdType.MESH
        )
    )
    pl.semaphore_wait(barrier, total - 1)

    mark_copy = [
        remote(marks, marks_in.at[a], k_send.at[a], k_recv.at[a], forward[a]) for a in range(2)
    ]
    border_copy = [
        remote(
            border.at[0, pl.ds(goes[a] * per, per)], border_in.at[a],
            m_send.at[a], m_recv.at[a], forward[a],
        )
        for a in range(2)
    ]
    field_copy = [
        [
            remote(
                rhs.at[:, part(c)], fields.at[2 + a, :, part(c)],
                f_send.at[a, c], f_recv.at[a, c], forward[a],
            )
            for c in range(chunks)
        ]
        for a in range(2)
    ]
    back_copy = [
        [
            remote(
                prods_out.at[a, :, part(c)], prods_in.at[a, :, part(c)],
                b_send.at[a, c], b_recv.at[a, c], backward[a],
            )
            for c in range(chunks)
        ]
        for a in range(2)
    ]
    image_copy = [
        [
            remote(
                images.at[0, :, part(c)], images.at[slot, :, part(c)],
                w_send.at[i, c], w_recv.at[i, c], where,
            )
            for c in range(chunks)
        ]
        for i, (slot, where) in enumerate(((2, right), (3, above), (1, partner)))
    ]
    field_pair = remote(rhs, fields.at[1], f_send.at[2, 0], f_recv.at[2, 0], partner)
    pair = remote(pair_out, pair_in, p_send, p_recv, partner)

    for a in range(2):
        given(has_next[a], lambda: border_copy[a].start())
    field_pair.start()
    loads[0].wait()
    loads[1].wait()
    for m in range(4 * per):
        marks[m : m + 1, :] = jnp.full((1, 128), send[0, m], jnp.int32).astype(jnp.float32)
        at = 4 * per + m
        marks[at : at + 1, :] = jnp.full((1, 128), rows[0, m], jnp.int32).astype(jnp.float32)
    for a in range(2):
        given(has_next[a], lambda: mark_copy[a].start())

    loads[2].wait()
    loads[3].wait()
    for i in range(nb):
        for j in range(nb):
            own = jnp.zeros((bs, bs), jnp.float32)
            far = jnp.zeros((bs, bs), jnp.float32)
            for k in range(nnz):
                block = local_v[i, k]
                col = cols[i, k]
                own = own + jnp.where(col == nd * nb + j, 1.0, 0.0) * block
                far = far + jnp.where(col == (1 - nd) * nb + j, 1.0, 0.0) * block
            prec[0, i * bs : (i + 1) * bs, j * bs : (j + 1) * bs] = own
            pair_out[i * bs : (i + 1) * bs, j * bs : (j + 1) * bs] = far
    pair.start()
    loads[4].wait()
    for m in range(4 * per):
        if m // per in came:
            turned[m] = border_v[m].T
    for a in range(2):
        given(has_next[a], lambda: border_copy[a].wait_send())
        given(has_next[a], lambda: field_copy[a][0].start())
    prec[0] = prec[0] + prec[0].T
    loads[5].wait()

    def weights(a, i, j):
        turn, opp = came[a], goes[a]
        for s in range(per):
            m, n = turn * per + s, opp * per + s
            at = 4 * per + n
            yield (
                jnp.where(rows[0, m] == i, 1.0, 0.0)
                * jnp.where(marks_in[a, m : m + 1, :] == float(j), 1.0, 0.0),
                jnp.where(send[0, n] == i, 1.0, 0.0)
                * jnp.where(marks_in[a, at : at + 1, :] == float(j), 1.0, 0.0),
                m,
                s,
            )

    def couple(a):
        mark_copy[a].wait_recv()
        border_copy[a].wait_recv()
        for i in range(nb):
            for j in range(nb):
                block = jnp.zeros((bs, bs), jnp.float32)
                for own, back, m, s in weights(a, i, j):
                    block = block + own * turned[m] + back * border_in[a, s]
                prec[4 + a, j * bs : (j + 1) * bs, i * bs : (i + 1) * bs] = block
        prods_out[a, :, span(0)] = mm(prec[4 + a], fields[0, :, span(0)])
        back_copy[a][0].start()

    def finish(a):
        for c in range(1, chunks):
            prods_out[a, :, span(c)] = mm(prec[4 + a], fields[0, :, span(c)])
            back_copy[a][c].start()

    def uncouple(a):
        prec[2 + a] = prec[4 + a].T

    given(has_last[0], lambda: couple(0))
    given(has_last[1], lambda: couple(1))
    for c in range(1, chunks):
        for a in range(2):
            given(has_next[a], lambda: field_copy[a][c].start())
    given(has_last[0], lambda: finish(0))
    given(has_last[1], lambda: finish(1))
    given(has_last[0], lambda: uncouple(0))
    given(has_last[1], lambda: uncouple(1))

    loads[6].wait()
    eye = lax.broadcasted_iota(jnp.int32, (size, size), 0) == lax.broadcasted_iota(
        jnp.int32, (size, size), 1
    )
    column = jnp.sum(
        jnp.where(eye, jnp.broadcast_to(diag[...], (size, size)), 0.0), axis=1, keepdims=True
    )
    work[...] = column * fields[0] + mm(prec[0], fields[0])
    pair.wait()
    prec[1] = pair_out[...] + pair_in[...].T
    field_pair.wait()
    work[...] += mm(prec[1], fields[1])

    for c in range(chunks):

        def from_last(a):
            field_copy[a][c].wait_recv()
            work[:, span(c)] += mm(prec[2 + a], fields[2 + a, :, span(c)])

        def from_next(a):
            back_copy[a][c].wait_recv()
            work[:, span(c)] += prods_in[a, :, span(c)]

        for a in (1, 0):
            given(has_last[a], lambda: from_last(a))
            given(has_next[a], lambda: from_next(a))
        images[0, :, span(c)] = work[:, span(c)]
        image_copy[0][c].start()
        given(high, lambda: image_copy[1][c].start())
        image_copy[2][c].start()

    def share(phase, first, second):
        sums[phase, me, 0:1, :] = first
        sums[phase, me, 1:2, :] = second
        over_peers(
            lambda step: remote(
                sums.at[phase, me], sums.at[phase, me], s_send.at[phase], s_recv.at[phase],
                peer(step),
            ).start()
        )

    def collect(phase):
        every = sums.at[phase, pl.ds(0, total - 1)]
        done = remote(every, every, s_send.at[phase], s_recv.at[phase], partner)
        done.wait_send()
        done.wait_recv()
        both = jnp.sum(sums[phase], axis=0)
        return both[0:1, :], both[1:2, :]

    share(0, column_sum(fields[0] * fields[0]), column_sum(fields[0] * images[0]))
    norm, curve = collect(0)
    alpha = norm / curve

    out[...] = fields[0] - alpha * images[0]
    work[...] = column * out[...] + mm(prec[0], out[...])
    for c in range(chunks):

        def quad_last(a):
            image_copy[a][c].wait_recv()
            behind = fields[2 + a, :, span(c)] - alpha[:, span(c)] * images[2 + a, :, span(c)]
            work[:, span(c)] += 2.0 * mm(prec[2 + a], behind)

        image_copy[2][c].wait_recv()
        across = fields[1, :, span(c)] - alpha[:, span(c)] * images[1, :, span(c)]
        work[:, span(c)] += mm(prec[1], across)
        for a in (1, 0):
            given(has_last[a], lambda: quad_last(a))
    share(1, column_sum(out[...] * out[...]), column_sum(out[...] * work[...]))

    for a in range(2):
        given(has_next[a], lambda: mark_copy[a].wait_send())
        for c in range(chunks):
            given(has_next[a], lambda: field_copy[a][c].wait_send())
            given(has_last[a], lambda: back_copy[a][c].wait_send())
            given(has_next[a], lambda: image_copy[a][c].wait_send())
    for c in range(chunks):
        image_copy[2][c].wait_send()

    norm_next, quad = collect(1)
    ratio = norm_next / norm
    alpha_next = norm_next / (quad - ratio * norm_next / alpha)
    out[...] = (alpha + alpha_next * ratio) * fields[0] + alpha_next * out[...]


def shards(sizes, right_side, node_diag, local_coup, block_cols, border_coup, border_send, border_rows):
    size, width = right_side.shape
    nb, nnz, bs, _ = local_coup.shape
    slots = border_coup.shape[1]
    per = slots // 4
    total = sizes[0] * sizes[1] * sizes[2]
    chunks = width // CHUNK
    hbm = pl.BlockSpec(memory_space=pltpu.HBM)
    f32 = jnp.float32
    dma = pltpu.SemaphoreType.DMA
    return pl.pallas_call(
        functools.partial(kernel, sizes),
        out_shape=jax.ShapeDtypeStruct((size, width), f32),
        in_specs=[hbm] * 7,
        out_specs=pl.BlockSpec(memory_space=pltpu.VMEM),
        scratch_shapes=[
            pltpu.VMEM((4, size, width), f32),
            pltpu.VMEM((4, size, width), f32),
            pltpu.VMEM((2, size, width), f32),
            pltpu.VMEM((2, size, width), f32),
            pltpu.VMEM((nb, nnz, bs, bs), f32),
            pltpu.VMEM((slots, bs, bs), f32),
            pltpu.VMEM((2, per, bs, bs), f32),
            pltpu.VMEM((size, size), f32),
            pltpu.VMEM((size, size), f32),
            pltpu.VMEM((2 * slots, 128), f32),
            pltpu.VMEM((2, 2 * slots, 128), f32),
            pltpu.VMEM((6, size, size), f32),
            pltpu.VMEM((slots, bs, bs), f32),
            pltpu.VMEM((size, width), f32),
            pltpu.VMEM((2, total, 2, width), f32),
            pltpu.VMEM((1, size), f32),
            pltpu.SMEM((nb, nnz), jnp.int32),
            pltpu.SMEM((1, slots), jnp.int32),
            pltpu.SMEM((1, slots), jnp.int32),
            dma((7,)), dma((3, chunks)), dma((3, chunks)), dma((2,)), dma((2,)), dma((2,)), dma((2,)),
            dma, dma, dma((2, chunks)), dma((2, chunks)), dma((3, chunks)), dma((3, chunks)),
            dma((2,)), dma((2,)),
        ],
        compiler_params=pltpu.CompilerParams(
            collective_id=0, has_side_effects=True
        ),
    )(
        right_side, node_diag.reshape(1, size), local_coup, block_cols, border_coup,
        border_send, border_rows,
    )


def solution(mesh):
    in_specs = (
        P(("var", "gx", "gy", "nd"), None),
        P(("var", "gx", "gy", "nd")),
        P(("var", "gx", "gy", "nd"), None, None, None),
        P(("gx", "gy", "nd"), None),
        P(("var", "gx", "gy", "nd"), None, None, None),
        P(("gx", "gy", "nd"), None),
        P(("gx", "gy", "nd"), None),
    )
    out_specs = P(("var", "gx", "gy", "nd"), None)
    sizes = tuple(mesh.shape[axis] for axis in ("gx", "gy", "nd"))
    return jax.shard_map(
        functools.partial(shards, sizes), mesh=mesh, in_specs=in_specs, out_specs=out_specs,
        check_vma=False,
    )
```

```python
import functools

import jax
import jax.numpy as jnp
from jax import lax
from jax.experimental import pallas as pl
from jax.experimental.pallas import tpu as pltpu
from jax.sharding import PartitionSpec as P

LEFT, RIGHT, DOWN, UP = range(4)
CHUNK = 128


def halves(a):
    high = a.astype(jnp.bfloat16)
    return high, (a - high.astype(jnp.float32)).astype(jnp.bfloat16)


def dot(a, b):
    return jnp.dot(a, b, preferred_element_type=jnp.float32)


def mm(a, b):
    a_high, a_low = halves(a)
    b_high, b_low = halves(b)
    return dot(a_high, b_high) + (dot(a_high, b_low) + dot(a_low, b_high))


def column_sum(a):
    return jnp.sum(a, axis=0, keepdims=True)


def kernel(
    sizes,
    rhs, diag_hbm, local, cols_hbm, border, send_hbm, rows_hbm,
    left_over, scale, scale_left,
    fields, images, prods_out, prods_in, local_v, border_v, border_in, pair_out, pair_in,
    marks, marks_in, prec, turned, work, residual, sums, diag, cols, send, rows,
    load_sem, f_send, f_recv, m_send, m_recv, k_send, k_recv, p_send, p_recv,
    b_send, b_recv, w_send, w_recv, s_send, s_recv,
):
    nx, ny, nn = sizes
    total = nx * ny * nn
    nb, nnz, bs, _ = local_v.shape
    per = border_v.shape[0] // 4
    size, width = left_over.shape
    chunks = width // CHUNK
    gx, gy, nd = lax.axis_index("gx"), lax.axis_index("gy"), lax.axis_index("nd")
    me = (gx * ny + gy) * nn + nd
    low = gy > 0
    high = gy < ny - 1
    left = {"gx": lax.rem(gx + nx - 1, nx)}
    right = {"gx": lax.rem(gx + 1, nx)}
    below = {"gy": jnp.maximum(gy - 1, 0)}
    above = {"gy": jnp.minimum(gy + 1, ny - 1)}
    partner = {"nd": 1 - nd}
    forward = (right, above)
    backward = (left, below)
    has_next = (None, high)
    has_last = (None, low)
    came = (LEFT, DOWN)
    goes = (RIGHT, UP)

    def given(condition, body):
        if condition is None:
            body()
        else:
            pl.when(condition)(body)

    def part(c):
        return pl.ds(c * CHUNK, CHUNK)

    def span(c):
        return slice(c * CHUNK, (c + 1) * CHUNK)

    def peer(step):
        other = lax.rem(me + step, total)
        return {"gx": other // (ny * nn), "gy": lax.rem(other // nn, ny), "nd": lax.rem(other, nn)}

    def over_peers(body):
        if total <= 16:
            xs = [lax.rem(gx + k, nx) for k in range(nx)]
            ys = [lax.rem(gy + k, ny) for k in range(ny)]
            ns = [lax.rem(nd + k, nn) for k in range(nn)]
            for i in range(nx):
                for j in range(ny):
                    for k in range(nn):
                        if (i, j, k) != (0, 0, 0):
                            body({"gx": xs[i], "gy": ys[j], "nd": ns[k]})
        else:
            lax.fori_loop(1, total, lambda step, _: (body(peer(step)), 0)[1], 0)

    def remote(src, dst, ssem, rsem, where):
        return pltpu.make_async_remote_copy(
            src_ref=src, dst_ref=dst, send_sem=ssem, recv_sem=rsem,
            device_id=where, device_id_type=pl.DeviceIdType.MESH,
        )

    pairs = (
        (send_hbm, send), (rows_hbm, rows), (cols_hbm, cols), (local, local_v),
        (border.at[0], border_v), (rhs, fields.at[0]), (diag_hbm, diag),
    )
    loads = [pltpu.make_async_copy(src, dst, load_sem.at[i]) for i, (src, dst) in enumerate(pairs)]
    for load in loads:
        load.start()

    barrier = pltpu.get_barrier_semaphore()
    over_peers(
        lambda other: pl.semaphore_signal(
            barrier, inc=1, device_id=other, device_id_type=pl.DeviceIdType.MESH
        )
    )
    pl.semaphore_wait(barrier, total - 1)

    mark_copy = [
        remote(marks, marks_in.at[a], k_send.at[a], k_recv.at[a], forward[a]) for a in range(2)
    ]
    border_copy = [
        remote(
            border.at[0, pl.ds(goes[a] * per, per)], border_in.at[a],
            m_send.at[a], m_recv.at[a], forward[a],
        )
        for a in range(2)
    ]
    field_copy = [
        [
            remote(
                rhs.at[:, part(c)], fields.at[2 + a, :, part(c)],
                f_send.at[a, c], f_recv.at[a, c], forward[a],
            )
            for c in range(chunks)
        ]
        for a in range(2)
    ]
    back_copy = [
        [
            remote(
                prods_out.at[a, :, part(c)], prods_in.at[a, :, part(c)],
                b_send.at[a, c], b_recv.at[a, c], backward[a],
            )
            for c in range(chunks)
        ]
        for a in range(2)
    ]
    image_copy = [
        [
            remote(
                images.at[0, :, part(c)], images.at[slot, :, part(c)],
                w_send.at[i, c], w_recv.at[i, c], where,
            )
            for c in range(chunks)
        ]
        for i, (slot, where) in enumerate(((2, right), (3, above), (1, partner)))
    ]
    field_pair = remote(rhs, fields.at[1], f_send.at[2, 0], f_recv.at[2, 0], partner)
    pair = remote(pair_out, pair_in, p_send, p_recv, partner)

    for a in range(2):
        given(has_next[a], lambda: border_copy[a].start())
    for a in range(2):
        given(has_next[a], lambda: field_copy[a][0].start())
    field_pair.start()
    loads[0].wait()
    loads[1].wait()
    for m in range(4 * per):
        marks[m : m + 1, :] = jnp.full((1, 128), send[0, m], jnp.int32).astype(jnp.float32)
        at = 4 * per + m
        marks[at : at + 1, :] = jnp.full((1, 128), rows[0, m], jnp.int32).astype(jnp.float32)
    for a in range(2):
        given(has_next[a], lambda: mark_copy[a].start())

    loads[2].wait()
    loads[3].wait()
    for i in range(nb):
        for j in range(nb):
            own = jnp.zeros((bs, bs), jnp.float32)
            far = jnp.zeros((bs, bs), jnp.float32)
            for k in range(nnz):
                block = local_v[i, k]
                col = cols[i, k]
                own = own + jnp.where(col == nd * nb + j, 1.0, 0.0) * block
                far = far + jnp.where(col == (1 - nd) * nb + j, 1.0, 0.0) * block
            prec[0, i * bs : (i + 1) * bs, j * bs : (j + 1) * bs] = own
            pair_out[i * bs : (i + 1) * bs, j * bs : (j + 1) * bs] = far
    pair.start()
    loads[4].wait()
    for m in range(4 * per):
        if m // per in came:
            turned[m] = border_v[m].T
    prec[0] = prec[0] + prec[0].T
    loads[5].wait()

    def weights(a, i, j):
        turn, opp = came[a], goes[a]
        for s in range(per):
            m, n = turn * per + s, opp * per + s
            at = 4 * per + n
            yield (
                jnp.where(rows[0, m] == i, 1.0, 0.0)
                * jnp.where(marks_in[a, m : m + 1, :] == float(j), 1.0, 0.0),
                jnp.where(send[0, n] == i, 1.0, 0.0)
                * jnp.where(marks_in[a, at : at + 1, :] == float(j), 1.0, 0.0),
                m,
                s,
            )

    def couple(a):
        mark_copy[a].wait_recv()
        border_copy[a].wait_recv()
        for i in range(nb):
            for j in range(nb):
                block = jnp.zeros((bs, bs), jnp.float32)
                for own, back, m, s in weights(a, i, j):
                    block = block + own * turned[m] + back * border_in[a, s]
                prec[4 + a, j * bs : (j + 1) * bs, i * bs : (i + 1) * bs] = block
        prods_out[a, :, span(0)] = mm(prec[4 + a], fields[0, :, span(0)])
        back_copy[a][0].start()

    def finish(a):
        for c in range(1, chunks):
            prods_out[a, :, span(c)] = mm(prec[4 + a], fields[0, :, span(c)])
            back_copy[a][c - 1].wait_send()
            back_copy[a][c].start()

    def uncouple(a):
        prec[2 + a] = prec[4 + a].T

    given(has_last[0], lambda: couple(0))
    given(has_last[1], lambda: couple(1))
    for c in range(1, chunks):
        for a in range(2):
            given(has_next[a], lambda: field_copy[a][c].start())
    given(has_last[0], lambda: uncouple(0))
    given(has_last[1], lambda: uncouple(1))

    loads[6].wait()
    eye = lax.broadcasted_iota(jnp.int32, (size, size), 0) == lax.broadcasted_iota(
        jnp.int32, (size, size), 1
    )
    column = jnp.sum(
        jnp.where(eye, jnp.broadcast_to(diag[...], (size, size)), 0.0), axis=1, keepdims=True
    )
    work[...] = column * fields[0] + mm(prec[0], fields[0])
    pair.wait()
    prec[1] = pair_out[...] + pair_in[...].T
    field_pair.wait()
    work[...] += mm(prec[1], fields[1])
    given(has_last[1], lambda: finish(1))
    given(has_last[0], lambda: finish(0))

    for c in range(chunks):

        def from_last(a):
            field_copy[a][c].wait_recv()
            work[:, span(c)] += mm(prec[2 + a], fields[2 + a, :, span(c)])

        def from_next(a):
            back_copy[a][c].wait_recv()
            work[:, span(c)] += prods_in[a, :, span(c)]

        for a in (1, 0):
            given(has_last[a], lambda: from_last(a))
            given(has_next[a], lambda: from_next(a))
        images[0, :, span(c)] = work[:, span(c)]
        image_copy[0][c].start()
        given(high, lambda: image_copy[1][c].start())
        image_copy[2][c].start()

    def share(phase, first, second):
        sums[phase, me, 0:1, :] = first
        sums[phase, me, 1:2, :] = second
        over_peers(
            lambda other: remote(
                sums.at[phase, me], sums.at[phase, me], s_send.at[phase], s_recv.at[phase],
                other,
            ).start()
        )

    def collect(phase):
        every = sums.at[phase, pl.ds(0, total - 1)]
        done = remote(every, every, s_send.at[phase], s_recv.at[phase], partner)
        done.wait_send()
        done.wait_recv()
        both = jnp.sum(sums[phase], axis=0)
        return both[0:1, :], both[1:2, :]

    share(0, column_sum(fields[0] * fields[0]), column_sum(fields[0] * images[0]))
    norm, curve = collect(0)
    alpha = norm / curve

    residual[...] = fields[0] - alpha * images[0]
    store = pltpu.make_async_copy(residual, left_over, load_sem.at[0])
    store.start()
    work[...] = column * residual[...] + mm(prec[0], residual[...])
    for c in range(chunks):

        def quad_last(a):
            image_copy[a][c].wait_recv()
            behind = fields[2 + a, :, span(c)] - alpha[:, span(c)] * images[2 + a, :, span(c)]
            work[:, span(c)] += 2.0 * mm(prec[2 + a], behind)

        image_copy[2][c].wait_recv()
        across = fields[1, :, span(c)] - alpha[:, span(c)] * images[1, :, span(c)]
        work[:, span(c)] += mm(prec[1], across)
        for a in (1, 0):
            given(has_last[a], lambda: quad_last(a))
    share(1, column_sum(residual[...] * residual[...]), column_sum(residual[...] * work[...]))

    for a in range(2):
        given(has_next[a], lambda: mark_copy[a].wait_send())
        given(has_next[a], lambda: border_copy[a].wait_send())
        given(has_last[a], lambda: back_copy[a][chunks - 1].wait_send())
        for c in range(chunks):
            given(has_next[a], lambda: field_copy[a][c].wait_send())
            given(has_next[a], lambda: image_copy[a][c].wait_send())
    for c in range(chunks):
        image_copy[2][c].wait_send()

    norm_next, quad = collect(1)
    ratio = norm_next / norm
    alpha_next = norm_next / (quad - ratio * norm_next / alpha)
    scale[...] = alpha + alpha_next * ratio
    scale_left[...] = alpha_next
    store.wait()


def shards(sizes, right_side, node_diag, local_coup, block_cols, border_coup, border_send, border_rows):
    size, width = right_side.shape
    nb, nnz, bs, _ = local_coup.shape
    slots = border_coup.shape[1]
    per = slots // 4
    total = sizes[0] * sizes[1] * sizes[2]
    chunks = width // CHUNK
    hbm = pl.BlockSpec(memory_space=pltpu.HBM)
    f32 = jnp.float32
    dma = pltpu.SemaphoreType.DMA
    left_over, scale, scale_left = pl.pallas_call(
        functools.partial(kernel, sizes),
        out_shape=(
            jax.ShapeDtypeStruct((size, width), f32),
            jax.ShapeDtypeStruct((1, width), f32),
            jax.ShapeDtypeStruct((1, width), f32),
        ),
        in_specs=[hbm] * 7,
        out_specs=(hbm,) + (pl.BlockSpec(memory_space=pltpu.VMEM),) * 2,
        scratch_shapes=[
            pltpu.VMEM((4, size, width), f32),
            pltpu.VMEM((4, size, width), f32),
            pltpu.VMEM((2, size, width), f32),
            pltpu.VMEM((2, size, width), f32),
            pltpu.VMEM((nb, nnz, bs, bs), f32),
            pltpu.VMEM((slots, bs, bs), f32),
            pltpu.VMEM((2, per, bs, bs), f32),
            pltpu.VMEM((size, size), f32),
            pltpu.VMEM((size, size), f32),
            pltpu.VMEM((2 * slots, 128), f32),
            pltpu.VMEM((2, 2 * slots, 128), f32),
            pltpu.VMEM((6, size, size), f32),
            pltpu.VMEM((slots, bs, bs), f32),
            pltpu.VMEM((size, width), f32),
            pltpu.VMEM((size, width), f32),
            pltpu.VMEM((2, total, 2, width), f32),
            pltpu.VMEM((1, size), f32),
            pltpu.SMEM((nb, nnz), jnp.int32),
            pltpu.SMEM((1, slots), jnp.int32),
            pltpu.SMEM((1, slots), jnp.int32),
            dma((7,)), dma((3, chunks)), dma((3, chunks)), dma((2,)), dma((2,)), dma((2,)), dma((2,)),
            dma, dma, dma((2, chunks)), dma((2, chunks)), dma((3, chunks)), dma((3, chunks)),
            dma((2,)), dma((2,)),
        ],
        compiler_params=pltpu.CompilerParams(
            collective_id=0, has_side_effects=True
        ),
    )(
        right_side, node_diag.reshape(1, size), local_coup, block_cols, border_coup,
        border_send, border_rows,
    )
    return scale * right_side + scale_left * left_over


def solution(mesh):
    in_specs = (
        P(("var", "gx", "gy", "nd"), None),
        P(("var", "gx", "gy", "nd")),
        P(("var", "gx", "gy", "nd"), None, None, None),
        P(("gx", "gy", "nd"), None),
        P(("var", "gx", "gy", "nd"), None, None, None),
        P(("gx", "gy", "nd"), None),
        P(("gx", "gy", "nd"), None),
    )
    out_specs = P(("var", "gx", "gy", "nd"), None)
    sizes = tuple(mesh.shape[axis] for axis in ("gx", "gy", "nd"))
    return jax.shard_map(
        functools.partial(shards, sizes), mesh=mesh, in_specs=in_specs, out_specs=out_specs,
        check_vma=False,
    )
```

```python
import functools

import jax
import jax.numpy as jnp
from jax import lax
from jax.experimental import pallas as pl
from jax.experimental.pallas import tpu as pltpu
from jax.sharding import PartitionSpec as P

LEFT, RIGHT, DOWN, UP = range(4)
CHUNK = 128


def halves(a):
    high = a.astype(jnp.bfloat16)
    return high, (a - high.astype(jnp.float32)).astype(jnp.bfloat16)


def dot(a, b):
    return jnp.dot(a, b, preferred_element_type=jnp.float32)


def mm(a, b):
    a_high, a_low = halves(a)
    b_high, b_low = halves(b)
    return dot(a_high, b_high) + (dot(a_high, b_low) + dot(a_low, b_high))


def column_sum(a):
    return jnp.sum(a, axis=0, keepdims=True)


def kernel(
    sizes,
    rhs, diag_hbm, local, cols_hbm, border, send_hbm, rows_hbm,
    out,
    fields, images, prods_out, prods_in, local_v, border_v, border_in, pair_out, pair_in,
    marks, marks_in, prec, turned, work, sums, diag, cols, send, rows,
    load_sem, f_send, f_recv, m_send, m_recv, k_send, k_recv, p_send, p_recv,
    b_send, b_recv, w_send, w_recv, s_send, s_recv,
):
    nx, ny, nn = sizes
    total = nx * ny * nn
    nb, nnz, bs, _ = local_v.shape
    per = border_v.shape[0] // 4
    size, width = out.shape
    chunks = width // CHUNK
    gx, gy, nd = lax.axis_index("gx"), lax.axis_index("gy"), lax.axis_index("nd")
    me = (gx * ny + gy) * nn + nd
    low = gy > 0
    high = gy < ny - 1
    left = {"gx": lax.rem(gx + nx - 1, nx)}
    right = {"gx": lax.rem(gx + 1, nx)}
    below = {"gy": jnp.maximum(gy - 1, 0)}
    above = {"gy": jnp.minimum(gy + 1, ny - 1)}
    partner = {"nd": 1 - nd}
    forward = (right, above)
    backward = (left, below)
    has_next = (None, high)
    has_last = (None, low)
    came = (LEFT, DOWN)
    goes = (RIGHT, UP)

    def given(condition, body):
        if condition is None:
            body()
        else:
            pl.when(condition)(body)

    def part(c):
        return pl.ds(c * CHUNK, CHUNK)

    def span(c):
        return slice(c * CHUNK, (c + 1) * CHUNK)

    def peer(step):
        other = lax.rem(me + step, total)
        return {"gx": other // (ny * nn), "gy": lax.rem(other // nn, ny), "nd": lax.rem(other, nn)}

    def over_peers(body):
        if total <= 16:
            xs = [lax.rem(gx + k, nx) for k in range(nx)]
            ys = [lax.rem(gy + k, ny) for k in range(ny)]
            ns = [lax.rem(nd + k, nn) for k in range(nn)]
            for i in range(nx):
                for j in range(ny):
                    for k in range(nn):
                        if (i, j, k) != (0, 0, 0):
                            body({"gx": xs[i], "gy": ys[j], "nd": ns[k]})
        else:
            lax.fori_loop(1, total, lambda step, _: (body(peer(step)), 0)[1], 0)

    def remote(src, dst, ssem, rsem, where):
        return pltpu.make_async_remote_copy(
            src_ref=src, dst_ref=dst, send_sem=ssem, recv_sem=rsem,
            device_id=where, device_id_type=pl.DeviceIdType.MESH,
        )

    pairs = (
        (send_hbm, send), (rows_hbm, rows), (cols_hbm, cols), (local, local_v),
        (border.at[0], border_v), (rhs, fields.at[0]), (diag_hbm, diag),
    )
    loads = [pltpu.make_async_copy(src, dst, load_sem.at[i]) for i, (src, dst) in enumerate(pairs)]
    for load in loads:
        load.start()

    barrier = pltpu.get_barrier_semaphore()
    over_peers(
        lambda other: pl.semaphore_signal(
            barrier, inc=1, device_id=other, device_id_type=pl.DeviceIdType.MESH
        )
    )
    pl.semaphore_wait(barrier, total - 1)

    mark_copy = [
        remote(marks, marks_in.at[a], k_send.at[a], k_recv.at[a], forward[a]) for a in range(2)
    ]
    border_copy = [
        remote(
            border.at[0, pl.ds(goes[a] * per, per)], border_in.at[a],
            m_send.at[a], m_recv.at[a], forward[a],
        )
        for a in range(2)
    ]
    field_copy = [
        [
            remote(
                rhs.at[:, part(c)], fields.at[2 + a, :, part(c)],
                f_send.at[a, c], f_recv.at[a, c], forward[a],
            )
            for c in range(chunks)
        ]
        for a in range(2)
    ]
    back_copy = [
        [
            remote(
                prods_out.at[a, :, part(c)], prods_in.at[a, :, part(c)],
                b_send.at[a, c], b_recv.at[a, c], backward[a],
            )
            for c in range(chunks)
        ]
        for a in range(2)
    ]
    image_copy = [
        [
            remote(
                images.at[0, :, part(c)], images.at[slot, :, part(c)],
                w_send.at[i, c], w_recv.at[i, c], where,
            )
            for c in range(chunks)
        ]
        for i, (slot, where) in enumerate(((2, right), (3, above), (1, partner)))
    ]
    field_pair = remote(rhs, fields.at[1], f_send.at[2, 0], f_recv.at[2, 0], partner)
    pair = remote(pair_out, pair_in, p_send, p_recv, partner)

    for a in range(2):
        given(has_next[a], lambda: border_copy[a].start())
    field_pair.start()
    loads[0].wait()
    loads[1].wait()
    for m in range(4 * per):
        marks[m : m + 1, :] = jnp.full((1, 128), send[0, m], jnp.int32).astype(jnp.float32)
        at = 4 * per + m
        marks[at : at + 1, :] = jnp.full((1, 128), rows[0, m], jnp.int32).astype(jnp.float32)
    for a in range(2):
        given(has_next[a], lambda: mark_copy[a].start())

    loads[2].wait()
    loads[3].wait()
    for i in range(nb):
        for j in range(nb):
            own = jnp.zeros((bs, bs), jnp.float32)
            far = jnp.zeros((bs, bs), jnp.float32)
            for k in range(nnz):
                block = local_v[i, k]
                col = cols[i, k]
                own = own + jnp.where(col == nd * nb + j, 1.0, 0.0) * block
                far = far + jnp.where(col == (1 - nd) * nb + j, 1.0, 0.0) * block
            prec[0, i * bs : (i + 1) * bs, j * bs : (j + 1) * bs] = own
            pair_out[i * bs : (i + 1) * bs, j * bs : (j + 1) * bs] = far
    pair.start()
    loads[4].wait()
    for m in range(4 * per):
        if m // per in came:
            turned[m] = border_v[m].T
    for a in range(2):
        given(has_next[a], lambda: border_copy[a].wait_send())
        given(has_next[a], lambda: field_copy[a][0].start())
    prec[0] = prec[0] + prec[0].T
    loads[5].wait()

    loads[6].wait()
    eye = lax.broadcasted_iota(jnp.int32, (size, size), 0) == lax.broadcasted_iota(
        jnp.int32, (size, size), 1
    )
    column = jnp.sum(
        jnp.where(eye, jnp.broadcast_to(diag[...], (size, size)), 0.0), axis=1, keepdims=True
    )
    work[...] = column * fields[0] + mm(prec[0], fields[0])
    def weights(a, i, j):
        turn, opp = came[a], goes[a]
        for s in range(per):
            m, n = turn * per + s, opp * per + s
            at = 4 * per + n
            yield (
                jnp.where(rows[0, m] == i, 1.0, 0.0)
                * jnp.where(marks_in[a, m : m + 1, :] == float(j), 1.0, 0.0),
                jnp.where(send[0, n] == i, 1.0, 0.0)
                * jnp.where(marks_in[a, at : at + 1, :] == float(j), 1.0, 0.0),
                m,
                s,
            )

    def couple(a):
        mark_copy[a].wait_recv()
        border_copy[a].wait_recv()
        for i in range(nb):
            for j in range(nb):
                block = jnp.zeros((bs, bs), jnp.float32)
                for own, back, m, s in weights(a, i, j):
                    block = block + own * turned[m] + back * border_in[a, s]
                prec[4 + a, j * bs : (j + 1) * bs, i * bs : (i + 1) * bs] = block
        prods_out[a, :, span(0)] = mm(prec[4 + a], fields[0, :, span(0)])
        back_copy[a][0].start()

    def follow(a, c):
        prods_out[a, :, span(c)] = mm(prec[4 + a], fields[0, :, span(c)])
        back_copy[a][c - 1].wait_send()
        back_copy[a][c].start()

    def uncouple(a):
        prec[2 + a] = prec[4 + a].T

    given(has_last[0], lambda: couple(0))
    given(has_last[1], lambda: couple(1))
    pair.wait()
    prec[1] = pair_out[...] + pair_in[...].T
    field_pair.wait()
    work[...] += mm(prec[1], fields[1])
    for c in range(1, chunks):
        for a in range(2):
            given(has_last[a], lambda: follow(a, c))
            given(has_next[a], lambda: field_copy[a][c].start())
    given(has_last[0], lambda: uncouple(0))
    given(has_last[1], lambda: uncouple(1))

    for c in range(chunks):

        def from_last(a):
            field_copy[a][c].wait_recv()
            work[:, span(c)] += mm(prec[2 + a], fields[2 + a, :, span(c)])

        def from_next(a):
            back_copy[a][c].wait_recv()
            work[:, span(c)] += prods_in[a, :, span(c)]

        for a in (1, 0):
            given(has_last[a], lambda: from_last(a))
            given(has_next[a], lambda: from_next(a))
        images[0, :, span(c)] = work[:, span(c)]
        image_copy[0][c].start()
        given(high, lambda: image_copy[1][c].start())
        image_copy[2][c].start()

    def share(phase, first, second):
        sums[phase, me, 0:1, :] = first
        sums[phase, me, 1:2, :] = second
        over_peers(
            lambda other: remote(
                sums.at[phase, me], sums.at[phase, me], s_send.at[phase], s_recv.at[phase],
                other,
            ).start()
        )

    def collect(phase):
        every = sums.at[phase, pl.ds(0, total - 1)]
        done = remote(every, every, s_send.at[phase], s_recv.at[phase], partner)
        done.wait_send()
        done.wait_recv()
        both = jnp.sum(sums[phase], axis=0)
        return both[0:1, :], both[1:2, :]

    share(0, column_sum(fields[0] * fields[0]), column_sum(fields[0] * images[0]))
    norm, curve = collect(0)
    alpha = norm / curve

    out[...] = fields[0] - alpha * images[0]
    work[...] = column * out[...] + mm(prec[0], out[...])
    for c in range(chunks):

        def quad_last(a):
            image_copy[a][c].wait_recv()
            behind = fields[2 + a, :, span(c)] - alpha[:, span(c)] * images[2 + a, :, span(c)]
            work[:, span(c)] += 2.0 * mm(prec[2 + a], behind)

        image_copy[2][c].wait_recv()
        across = fields[1, :, span(c)] - alpha[:, span(c)] * images[1, :, span(c)]
        work[:, span(c)] += mm(prec[1], across)
        for a in (1, 0):
            given(has_last[a], lambda: quad_last(a))
    share(1, column_sum(out[...] * out[...]), column_sum(out[...] * work[...]))

    for a in range(2):
        given(has_next[a], lambda: mark_copy[a].wait_send())
        given(has_last[a], lambda: back_copy[a][chunks - 1].wait_send())
        for c in range(chunks):
            given(has_next[a], lambda: field_copy[a][c].wait_send())
            given(has_next[a], lambda: image_copy[a][c].wait_send())
    for c in range(chunks):
        image_copy[2][c].wait_send()

    norm_next, quad = collect(1)
    ratio = norm_next / norm
    alpha_next = norm_next / (quad - ratio * norm_next / alpha)
    out[...] = (alpha + alpha_next * ratio) * fields[0] + alpha_next * out[...]


def shards(sizes, right_side, node_diag, local_coup, block_cols, border_coup, border_send, border_rows):
    size, width = right_side.shape
    nb, nnz, bs, _ = local_coup.shape
    slots = border_coup.shape[1]
    per = slots // 4
    total = sizes[0] * sizes[1] * sizes[2]
    chunks = width // CHUNK
    hbm = pl.BlockSpec(memory_space=pltpu.HBM)
    f32 = jnp.float32
    dma = pltpu.SemaphoreType.DMA
    return pl.pallas_call(
        functools.partial(kernel, sizes),
        out_shape=jax.ShapeDtypeStruct((size, width), f32),
        in_specs=[hbm] * 7,
        out_specs=pl.BlockSpec(memory_space=pltpu.VMEM),
        scratch_shapes=[
            pltpu.VMEM((4, size, width), f32),
            pltpu.VMEM((4, size, width), f32),
            pltpu.VMEM((2, size, width), f32),
            pltpu.VMEM((2, size, width), f32),
            pltpu.VMEM((nb, nnz, bs, bs), f32),
            pltpu.VMEM((slots, bs, bs), f32),
            pltpu.VMEM((2, per, bs, bs), f32),
            pltpu.VMEM((size, size), f32),
            pltpu.VMEM((size, size), f32),
            pltpu.VMEM((2 * slots, 128), f32),
            pltpu.VMEM((2, 2 * slots, 128), f32),
            pltpu.VMEM((6, size, size), f32),
            pltpu.VMEM((slots, bs, bs), f32),
            pltpu.VMEM((size, width), f32),
            pltpu.VMEM((2, total, 2, width), f32),
            pltpu.VMEM((1, size), f32),
            pltpu.SMEM((nb, nnz), jnp.int32),
            pltpu.SMEM((1, slots), jnp.int32),
            pltpu.SMEM((1, slots), jnp.int32),
            dma((7,)), dma((3, chunks)), dma((3, chunks)), dma((2,)), dma((2,)), dma((2,)), dma((2,)),
            dma, dma, dma((2, chunks)), dma((2, chunks)), dma((3, chunks)), dma((3, chunks)),
            dma((2,)), dma((2,)),
        ],
        compiler_params=pltpu.CompilerParams(
            collective_id=0, has_side_effects=True
        ),
    )(
        right_side, node_diag.reshape(1, size), local_coup, block_cols, border_coup,
        border_send, border_rows,
    )


def solution(mesh):
    in_specs = (
        P(("var", "gx", "gy", "nd"), None),
        P(("var", "gx", "gy", "nd")),
        P(("var", "gx", "gy", "nd"), None, None, None),
        P(("gx", "gy", "nd"), None),
        P(("var", "gx", "gy", "nd"), None, None, None),
        P(("gx", "gy", "nd"), None),
        P(("gx", "gy", "nd"), None),
    )
    out_specs = P(("var", "gx", "gy", "nd"), None)
    sizes = tuple(mesh.shape[axis] for axis in ("gx", "gy", "nd"))
    return jax.shard_map(
        functools.partial(shards, sizes), mesh=mesh, in_specs=in_specs, out_specs=out_specs,
        check_vma=False,
    )
```

```python
import functools

import jax
import jax.numpy as jnp
from jax import lax
from jax.experimental import pallas as pl
from jax.experimental.pallas import tpu as pltpu
from jax.sharding import PartitionSpec as P

LEFT, RIGHT, DOWN, UP = range(4)
CHUNK = 128


def halves(a):
    high = a.astype(jnp.bfloat16)
    return high, (a - high.astype(jnp.float32)).astype(jnp.bfloat16)


def dot(a, b):
    return jnp.dot(a, b, preferred_element_type=jnp.float32)


def mm(a, b):
    a_high, a_low = halves(a)
    b_high, b_low = halves(b)
    return dot(a_high, b_high) + (dot(a_high, b_low) + dot(a_low, b_high))


def column_sum(a):
    return jnp.sum(a, axis=0, keepdims=True)


def kernel(
    sizes,
    rhs, diag_hbm, local, cols_hbm, border, send_hbm, rows_hbm,
    out,
    fields, images, prods_out, prods_in, local_v, border_v, border_in, pair_out, pair_in,
    marks, marks_in, prec, turned, work, half, sums, diag, cols, send, rows,
    load_sem, f_send, f_recv, m_send, m_recv, k_send, k_recv, p_send, p_recv,
    b_send, b_recv, w_send, w_recv, s_send, s_recv,
):
    nx, ny, nn = sizes
    total = nx * ny * nn
    nb, nnz, bs, _ = local_v.shape
    per = border_v.shape[0] // 4
    size, width = out.shape
    chunks = width // CHUNK
    gx, gy, nd = lax.axis_index("gx"), lax.axis_index("gy"), lax.axis_index("nd")
    me = (gx * ny + gy) * nn + nd
    low = gy > 0
    high = gy < ny - 1
    left = {"gx": lax.rem(gx + nx - 1, nx)}
    right = {"gx": lax.rem(gx + 1, nx)}
    below = {"gy": jnp.maximum(gy - 1, 0)}
    above = {"gy": jnp.minimum(gy + 1, ny - 1)}
    partner = {"nd": 1 - nd}
    forward = (right, above)
    backward = (left, below)
    has_next = (None, high)
    has_last = (None, low)
    came = (LEFT, DOWN)
    goes = (RIGHT, UP)

    def given(condition, body):
        if condition is None:
            body()
        else:
            pl.when(condition)(body)

    def part(c):
        return pl.ds(c * CHUNK, CHUNK)

    def span(c):
        return slice(c * CHUNK, (c + 1) * CHUNK)

    def peer(step):
        other = lax.rem(me + step, total)
        return {"gx": other // (ny * nn), "gy": lax.rem(other // nn, ny), "nd": lax.rem(other, nn)}

    def over_peers(body):
        if total <= 16:
            xs = [lax.rem(gx + k, nx) for k in range(nx)]
            ys = [lax.rem(gy + k, ny) for k in range(ny)]
            ns = [lax.rem(nd + k, nn) for k in range(nn)]
            for i in range(nx):
                for j in range(ny):
                    for k in range(nn):
                        if (i, j, k) != (0, 0, 0):
                            body({"gx": xs[i], "gy": ys[j], "nd": ns[k]})
        else:
            lax.fori_loop(1, total, lambda step, _: (body(peer(step)), 0)[1], 0)

    def remote(src, dst, ssem, rsem, where):
        return pltpu.make_async_remote_copy(
            src_ref=src, dst_ref=dst, send_sem=ssem, recv_sem=rsem,
            device_id=where, device_id_type=pl.DeviceIdType.MESH,
        )

    pairs = (
        (send_hbm, send), (rows_hbm, rows), (cols_hbm, cols), (local, local_v),
        (border.at[0], border_v), (rhs, fields.at[0]), (diag_hbm, diag),
    )
    loads = [pltpu.make_async_copy(src, dst, load_sem.at[i]) for i, (src, dst) in enumerate(pairs)]
    for load in loads:
        load.start()

    barrier = pltpu.get_barrier_semaphore()
    over_peers(
        lambda other: pl.semaphore_signal(
            barrier, inc=1, device_id=other, device_id_type=pl.DeviceIdType.MESH
        )
    )
    pl.semaphore_wait(barrier, total - 1)

    mark_copy = [
        remote(marks, marks_in.at[a], k_send.at[a], k_recv.at[a], forward[a]) for a in range(2)
    ]
    border_copy = [
        remote(
            border.at[0, pl.ds(goes[a] * per, per)], border_in.at[a],
            m_send.at[a], m_recv.at[a], forward[a],
        )
        for a in range(2)
    ]
    field_copy = [
        [
            remote(
                rhs.at[:, part(c)], fields.at[2 + a, :, part(c)],
                f_send.at[a, c], f_recv.at[a, c], forward[a],
            )
            for c in range(chunks)
        ]
        for a in range(2)
    ]
    back_copy = [
        [
            remote(
                prods_out.at[a, :, part(c)], prods_in.at[a, :, part(c)],
                b_send.at[a, c], b_recv.at[a, c], backward[a],
            )
            for c in range(chunks)
        ]
        for a in range(2)
    ]
    image_copy = [
        [
            remote(
                images.at[0, :, part(c)], images.at[slot, :, part(c)],
                w_send.at[i, c], w_recv.at[i, c], where,
            )
            for c in range(chunks)
        ]
        for i, (slot, where) in enumerate(((2, right), (3, above), (1, partner)))
    ]
    field_pair = remote(rhs, fields.at[1], f_send.at[2, 0], f_recv.at[2, 0], partner)
    pair = remote(pair_out, pair_in, p_send, p_recv, partner)

    for a in range(2):
        given(has_next[a], lambda: border_copy[a].start())
    field_pair.start()
    loads[0].wait()
    loads[1].wait()
    for m in range(4 * per):
        marks[m : m + 1, :] = jnp.full((1, 128), send[0, m], jnp.int32).astype(jnp.float32)
        at = 4 * per + m
        marks[at : at + 1, :] = jnp.full((1, 128), rows[0, m], jnp.int32).astype(jnp.float32)
    for a in range(2):
        given(has_next[a], lambda: mark_copy[a].start())

    loads[2].wait()
    loads[3].wait()
    for i in range(nb):
        for j in range(nb):
            own = jnp.zeros((bs, bs), jnp.float32)
            far = jnp.zeros((bs, bs), jnp.float32)
            for k in range(nnz):
                block = local_v[i, k]
                col = cols[i, k]
                own = own + jnp.where(col == nd * nb + j, 1.0, 0.0) * block
                far = far + jnp.where(col == (1 - nd) * nb + j, 1.0, 0.0) * block
            prec[0, i * bs : (i + 1) * bs, j * bs : (j + 1) * bs] = own
            pair_out[i * bs : (i + 1) * bs, j * bs : (j + 1) * bs] = far
    pair.start()
    loads[4].wait()
    for m in range(4 * per):
        if m // per in came:
            turned[m] = border_v[m].T
    for a in range(2):
        given(has_next[a], lambda: border_copy[a].wait_send())
        given(has_next[a], lambda: field_copy[a][0].start())
    prec[0] = prec[0] + prec[0].T
    loads[5].wait()

    loads[6].wait()
    eye = lax.broadcasted_iota(jnp.int32, (size, size), 0) == lax.broadcasted_iota(
        jnp.int32, (size, size), 1
    )
    column = jnp.sum(
        jnp.where(eye, jnp.broadcast_to(diag[...], (size, size)), 0.0), axis=1, keepdims=True
    )
    half[...] = mm(prec[0], fields[0])

    def weights(a, i, j):
        turn, opp = came[a], goes[a]
        for s in range(per):
            m, n = turn * per + s, opp * per + s
            at = 4 * per + n
            yield (
                jnp.where(rows[0, m] == i, 1.0, 0.0)
                * jnp.where(marks_in[a, m : m + 1, :] == float(j), 1.0, 0.0),
                jnp.where(send[0, n] == i, 1.0, 0.0)
                * jnp.where(marks_in[a, at : at + 1, :] == float(j), 1.0, 0.0),
                m,
                s,
            )

    def couple(a):
        mark_copy[a].wait_recv()
        border_copy[a].wait_recv()
        for i in range(nb):
            for j in range(nb):
                block = jnp.zeros((bs, bs), jnp.float32)
                for own, back, m, s in weights(a, i, j):
                    block = block + own * turned[m] + back * border_in[a, s]
                prec[4 + a, j * bs : (j + 1) * bs, i * bs : (i + 1) * bs] = block
        prods_out[a, :, span(0)] = mm(prec[4 + a], fields[0, :, span(0)])
        back_copy[a][0].start()

    def follow(a, c):
        prods_out[a, :, span(c)] = mm(prec[4 + a], fields[0, :, span(c)])
        back_copy[a][c - 1].wait_send()
        back_copy[a][c].start()

    def uncouple(a):
        prec[2 + a] = prec[4 + a].T

    given(has_last[0], lambda: couple(0))
    given(has_last[1], lambda: couple(1))
    pair.wait()
    prec[1] = pair_out[...] + pair_in[...].T
    field_pair.wait()
    half[...] += mm(prec[1], fields[1])
    work[...] = column * fields[0] + half[...]
    for c in range(1, chunks):
        for a in range(2):
            given(has_last[a], lambda: follow(a, c))
            given(has_next[a], lambda: field_copy[a][c].start())
    given(has_last[0], lambda: uncouple(0))
    given(has_last[1], lambda: uncouple(1))

    for c in range(chunks):

        def from_last(a):
            field_copy[a][c].wait_recv()
            term = mm(prec[2 + a], fields[2 + a, :, span(c)])
            work[:, span(c)] += term
            half[:, span(c)] += 2.0 * term

        def from_next(a):
            back_copy[a][c].wait_recv()
            work[:, span(c)] += prods_in[a, :, span(c)]

        for a in (1, 0):
            given(has_last[a], lambda: from_last(a))
            given(has_next[a], lambda: from_next(a))
        images[0, :, span(c)] = work[:, span(c)]
        image_copy[0][c].start()
        given(high, lambda: image_copy[1][c].start())
        image_copy[2][c].start()

    def share(phase, first, second):
        sums[phase, me, 0:1, :] = first
        sums[phase, me, 1:2, :] = second
        over_peers(
            lambda other: remote(
                sums.at[phase, me], sums.at[phase, me], s_send.at[phase], s_recv.at[phase],
                other,
            ).start()
        )

    def collect(phase):
        every = sums.at[phase, pl.ds(0, total - 1)]
        done = remote(every, every, s_send.at[phase], s_recv.at[phase], partner)
        done.wait_send()
        done.wait_recv()
        both = jnp.sum(sums[phase], axis=0)
        return both[0:1, :], both[1:2, :]

    share(0, column_sum(fields[0] * fields[0]), column_sum(fields[0] * images[0]))

    work[...] = mm(prec[0], images[0])
    for c in range(chunks):

        def quad_last(a):
            image_copy[a][c].wait_recv()
            work[:, span(c)] += 2.0 * mm(prec[2 + a], images[2 + a, :, span(c)])

        image_copy[2][c].wait_recv()
        work[:, span(c)] += mm(prec[1], images[1, :, span(c)])
        for a in (1, 0):
            given(has_last[a], lambda: quad_last(a))

    norm, curve = collect(0)
    alpha = norm / curve
    out[...] = fields[0] - alpha * images[0]
    work[...] = column * out[...] + (half[...] - alpha * work[...])
    share(1, column_sum(out[...] * out[...]), column_sum(out[...] * work[...]))

    for a in range(2):
        given(has_next[a], lambda: mark_copy[a].wait_send())
        given(has_last[a], lambda: back_copy[a][chunks - 1].wait_send())
        for c in range(chunks):
            given(has_next[a], lambda: field_copy[a][c].wait_send())
            given(has_next[a], lambda: image_copy[a][c].wait_send())
    for c in range(chunks):
        image_copy[2][c].wait_send()

    norm_next, quad = collect(1)
    ratio = norm_next / norm
    alpha_next = norm_next / (quad - ratio * norm_next / alpha)
    out[...] = (alpha + alpha_next * ratio) * fields[0] + alpha_next * out[...]


def shards(sizes, right_side, node_diag, local_coup, block_cols, border_coup, border_send, border_rows):
    size, width = right_side.shape
    nb, nnz, bs, _ = local_coup.shape
    slots = border_coup.shape[1]
    per = slots // 4
    total = sizes[0] * sizes[1] * sizes[2]
    chunks = width // CHUNK
    hbm = pl.BlockSpec(memory_space=pltpu.HBM)
    f32 = jnp.float32
    dma = pltpu.SemaphoreType.DMA
    return pl.pallas_call(
        functools.partial(kernel, sizes),
        out_shape=jax.ShapeDtypeStruct((size, width), f32),
        in_specs=[hbm] * 7,
        out_specs=pl.BlockSpec(memory_space=pltpu.VMEM),
        scratch_shapes=[
            pltpu.VMEM((4, size, width), f32),
            pltpu.VMEM((4, size, width), f32),
            pltpu.VMEM((2, size, width), f32),
            pltpu.VMEM((2, size, width), f32),
            pltpu.VMEM((nb, nnz, bs, bs), f32),
            pltpu.VMEM((slots, bs, bs), f32),
            pltpu.VMEM((2, per, bs, bs), f32),
            pltpu.VMEM((size, size), f32),
            pltpu.VMEM((size, size), f32),
            pltpu.VMEM((2 * slots, 128), f32),
            pltpu.VMEM((2, 2 * slots, 128), f32),
            pltpu.VMEM((6, size, size), f32),
            pltpu.VMEM((slots, bs, bs), f32),
            pltpu.VMEM((size, width), f32),
            pltpu.VMEM((size, width), f32),
            pltpu.VMEM((2, total, 2, width), f32),
            pltpu.VMEM((1, size), f32),
            pltpu.SMEM((nb, nnz), jnp.int32),
            pltpu.SMEM((1, slots), jnp.int32),
            pltpu.SMEM((1, slots), jnp.int32),
            dma((7,)), dma((3, chunks)), dma((3, chunks)), dma((2,)), dma((2,)), dma((2,)), dma((2,)),
            dma, dma, dma((2, chunks)), dma((2, chunks)), dma((3, chunks)), dma((3, chunks)),
            dma((2,)), dma((2,)),
        ],
        compiler_params=pltpu.CompilerParams(
            collective_id=0, has_side_effects=True
        ),
    )(
        right_side, node_diag.reshape(1, size), local_coup, block_cols, border_coup,
        border_send, border_rows,
    )


def solution(mesh):
    in_specs = (
        P(("var", "gx", "gy", "nd"), None),
        P(("var", "gx", "gy", "nd")),
        P(("var", "gx", "gy", "nd"), None, None, None),
        P(("gx", "gy", "nd"), None),
        P(("var", "gx", "gy", "nd"), None, None, None),
        P(("gx", "gy", "nd"), None),
        P(("gx", "gy", "nd"), None),
    )
    out_specs = P(("var", "gx", "gy", "nd"), None)
    sizes = tuple(mesh.shape[axis] for axis in ("gx", "gy", "nd"))
    return jax.shard_map(
        functools.partial(shards, sizes), mesh=mesh, in_specs=in_specs, out_specs=out_specs,
        check_vma=False,
    )
```

```python
import functools

import jax
import jax.numpy as jnp
from jax import lax
from jax.experimental import pallas as pl
from jax.experimental.pallas import tpu as pltpu
from jax.sharding import PartitionSpec as P

LEFT, RIGHT, DOWN, UP = range(4)
CHUNK = 128
PIECES = 4


def halves(a):
    high = a.astype(jnp.bfloat16)
    return high, (a - high.astype(jnp.float32)).astype(jnp.bfloat16)


def dot(a, b):
    return jnp.dot(a, b, preferred_element_type=jnp.float32)


def mm(a, b):
    a_high, a_low = halves(a)
    b_high, b_low = halves(b)
    width = b.shape[1]
    both = dot(a_high, jnp.concatenate([b_high, b_low], axis=1))
    return both[:, :width] + (both[:, width:] + dot(a_low, b_high))


def hand_over(found, out, sems):
    rows = out.shape[0] // PIECES
    copies = [
        pltpu.make_async_copy(
            found.at[pl.ds(i * rows, rows)], out.at[pl.ds(i * rows, rows)], sems.at[i]
        )
        for i in range(PIECES)
    ]
    for copy in copies:
        copy.start()
    for copy in copies:
        copy.wait()


def column_sum(a):
    return jnp.sum(a, axis=0, keepdims=True)


def kernel(
    sizes,
    rhs, diag_hbm, local, cols_hbm, border, send_hbm, rows_hbm,
    out,
    fields, images, prods_out, prods_in, local_v, border_v, border_in, pair_out, pair_in,
    marks, marks_in, prec, turned, work, half, sums, diag, cols, send, rows,
    load_sem, f_send, f_recv, m_send, m_recv, k_send, k_recv, p_send, p_recv,
    b_send, b_recv, w_send, w_recv, s_send, s_recv,
):
    nx, ny, nn = sizes
    total = nx * ny * nn
    nb, nnz, bs, _ = local_v.shape
    per = border_v.shape[0] // 4
    size, width = out.shape
    chunks = width // CHUNK
    gx, gy, nd = lax.axis_index("gx"), lax.axis_index("gy"), lax.axis_index("nd")
    me = (gx * ny + gy) * nn + nd
    low = gy > 0
    high = gy < ny - 1
    left = {"gx": lax.rem(gx + nx - 1, nx)}
    right = {"gx": lax.rem(gx + 1, nx)}
    below = {"gy": jnp.maximum(gy - 1, 0)}
    above = {"gy": jnp.minimum(gy + 1, ny - 1)}
    partner = {"nd": 1 - nd}
    forward = (right, above)
    backward = (left, below)
    has_next = (None, high)
    has_last = (None, low)
    came = (LEFT, DOWN)
    goes = (RIGHT, UP)

    def given(condition, body):
        if condition is None:
            body()
        else:
            pl.when(condition)(body)

    def part(c):
        return pl.ds(c * CHUNK, CHUNK)

    def span(c):
        return slice(c * CHUNK, (c + 1) * CHUNK)

    def peer(step):
        other = lax.rem(me + step, total)
        return {"gx": other // (ny * nn), "gy": lax.rem(other // nn, ny), "nd": lax.rem(other, nn)}

    def over_peers(body):
        if total <= 16:
            xs = [lax.rem(gx + k, nx) for k in range(nx)]
            ys = [lax.rem(gy + k, ny) for k in range(ny)]
            ns = [lax.rem(nd + k, nn) for k in range(nn)]
            for i in range(nx):
                for j in range(ny):
                    for k in range(nn):
                        if (i, j, k) != (0, 0, 0):
                            body({"gx": xs[i], "gy": ys[j], "nd": ns[k]})
        else:
            lax.fori_loop(1, total, lambda step, _: (body(peer(step)), 0)[1], 0)

    def remote(src, dst, ssem, rsem, where):
        return pltpu.make_async_remote_copy(
            src_ref=src, dst_ref=dst, send_sem=ssem, recv_sem=rsem,
            device_id=where, device_id_type=pl.DeviceIdType.MESH,
        )

    pairs = (
        (send_hbm, send), (rows_hbm, rows), (cols_hbm, cols), (local, local_v),
        (border.at[0], border_v), (rhs, fields.at[0]), (diag_hbm, diag),
    )
    loads = [pltpu.make_async_copy(src, dst, load_sem.at[i]) for i, (src, dst) in enumerate(pairs)]
    for load in loads:
        load.start()

    barrier = pltpu.get_barrier_semaphore()
    over_peers(
        lambda other: pl.semaphore_signal(
            barrier, inc=1, device_id=other, device_id_type=pl.DeviceIdType.MESH
        )
    )
    pl.semaphore_wait(barrier, total - 1)

    mark_copy = [
        remote(marks, marks_in.at[a], k_send.at[a], k_recv.at[a], forward[a]) for a in range(2)
    ]
    border_copy = [
        remote(
            border.at[0, pl.ds(goes[a] * per, per)], border_in.at[a],
            m_send.at[a], m_recv.at[a], forward[a],
        )
        for a in range(2)
    ]
    field_copy = [
        [
            remote(
                rhs.at[:, part(c)], fields.at[2 + a, :, part(c)],
                f_send.at[a, c], f_recv.at[a, c], forward[a],
            )
            for c in range(chunks)
        ]
        for a in range(2)
    ]
    back_copy = [
        [
            remote(
                prods_out.at[a, :, part(c)], prods_in.at[a, :, part(c)],
                b_send.at[a, c], b_recv.at[a, c], backward[a],
            )
            for c in range(chunks)
        ]
        for a in range(2)
    ]
    image_copy = [
        [
            remote(
                images.at[0, :, part(c)], images.at[slot, :, part(c)],
                w_send.at[i, c], w_recv.at[i, c], where,
            )
            for c in range(chunks)
        ]
        for i, (slot, where) in enumerate(((2, right), (3, above), (1, partner)))
    ]
    field_pair = remote(rhs, fields.at[1], f_send.at[2, 0], f_recv.at[2, 0], partner)
    pair = remote(pair_out, pair_in, p_send, p_recv, partner)

    for a in range(2):
        given(has_next[a], lambda: border_copy[a].start())
    field_pair.start()
    loads[0].wait()
    loads[1].wait()
    for m in range(4 * per):
        marks[m : m + 1, :] = jnp.full((1, 128), send[0, m], jnp.int32).astype(jnp.float32)
        at = 4 * per + m
        marks[at : at + 1, :] = jnp.full((1, 128), rows[0, m], jnp.int32).astype(jnp.float32)
    for a in range(2):
        given(has_next[a], lambda: mark_copy[a].start())

    loads[2].wait()
    loads[3].wait()
    for i in range(nb):
        for j in range(nb):
            own = jnp.zeros((bs, bs), jnp.float32)
            far = jnp.zeros((bs, bs), jnp.float32)
            for k in range(nnz):
                block = local_v[i, k]
                col = cols[i, k]
                own = own + jnp.where(col == nd * nb + j, 1.0, 0.0) * block
                far = far + jnp.where(col == (1 - nd) * nb + j, 1.0, 0.0) * block
            prec[0, i * bs : (i + 1) * bs, j * bs : (j + 1) * bs] = own
            pair_out[i * bs : (i + 1) * bs, j * bs : (j + 1) * bs] = far
    pair.start()
    loads[4].wait()
    for m in range(4 * per):
        if m // per in came:
            turned[m] = border_v[m].T
    for a in range(2):
        given(has_next[a], lambda: border_copy[a].wait_send())
        given(has_next[a], lambda: field_copy[a][0].start())
    prec[0] = prec[0] + prec[0].T
    loads[5].wait()

    loads[6].wait()
    eye = lax.broadcasted_iota(jnp.int32, (size, size), 0) == lax.broadcasted_iota(
        jnp.int32, (size, size), 1
    )
    column = jnp.sum(
        jnp.where(eye, jnp.broadcast_to(diag[...], (size, size)), 0.0), axis=1, keepdims=True
    )
    half[...] = mm(prec[0], fields[0])

    def weights(a, i, j):
        turn, opp = came[a], goes[a]
        for s in range(per):
            m, n = turn * per + s, opp * per + s
            at = 4 * per + n
            yield (
                jnp.where(rows[0, m] == i, 1.0, 0.0)
                * jnp.where(marks_in[a, m : m + 1, :] == float(j), 1.0, 0.0),
                jnp.where(send[0, n] == i, 1.0, 0.0)
                * jnp.where(marks_in[a, at : at + 1, :] == float(j), 1.0, 0.0),
                m,
                s,
            )

    def couple(a):
        mark_copy[a].wait_recv()
        border_copy[a].wait_recv()
        for i in range(nb):
            for j in range(nb):
                block = jnp.zeros((bs, bs), jnp.float32)
                for own, back, m, s in weights(a, i, j):
                    block = block + own * turned[m] + back * border_in[a, s]
                prec[4 + a, j * bs : (j + 1) * bs, i * bs : (i + 1) * bs] = block
        prods_out[a, :, span(0)] = mm(prec[4 + a], fields[0, :, span(0)])
        back_copy[a][0].start()

    def follow(a, c):
        prods_out[a, :, span(c)] = mm(prec[4 + a], fields[0, :, span(c)])
        back_copy[a][c - 1].wait_send()
        back_copy[a][c].start()

    def uncouple(a):
        prec[2 + a] = prec[4 + a].T

    given(has_last[0], lambda: couple(0))
    given(has_last[1], lambda: couple(1))
    pair.wait()
    prec[1] = pair_out[...] + pair_in[...].T
    field_pair.wait()
    half[...] += mm(prec[1], fields[1])
    work[...] = column * fields[0] + half[...]
    for c in range(1, chunks):
        for a in range(2):
            given(has_last[a], lambda: follow(a, c))
            given(has_next[a], lambda: field_copy[a][c].start())
    given(has_last[0], lambda: uncouple(0))
    given(has_last[1], lambda: uncouple(1))

    for c in range(chunks):

        def from_last(a):
            field_copy[a][c].wait_recv()
            term = mm(prec[2 + a], fields[2 + a, :, span(c)])
            work[:, span(c)] += term
            half[:, span(c)] += 2.0 * term

        def from_next(a):
            back_copy[a][c].wait_recv()
            work[:, span(c)] += prods_in[a, :, span(c)]

        for a in (1, 0):
            given(has_last[a], lambda: from_last(a))
            given(has_next[a], lambda: from_next(a))
        images[0, :, span(c)] = work[:, span(c)]
        image_copy[0][c].start()
        given(high, lambda: image_copy[1][c].start())
        image_copy[2][c].start()

    def share(phase, first, second):
        sums[phase, me, 0:1, :] = first
        sums[phase, me, 1:2, :] = second
        over_peers(
            lambda other: remote(
                sums.at[phase, me], sums.at[phase, me], s_send.at[phase], s_recv.at[phase],
                other,
            ).start()
        )

    def collect(phase):
        every = sums.at[phase, pl.ds(0, total - 1)]
        done = remote(every, every, s_send.at[phase], s_recv.at[phase], partner)
        done.wait_send()
        done.wait_recv()
        both = jnp.sum(sums[phase], axis=0)
        return both[0:1, :], both[1:2, :]

    share(0, column_sum(fields[0] * fields[0]), column_sum(fields[0] * images[0]))

    work[...] = mm(prec[0], images[0])
    for c in range(chunks):

        def quad_last(a):
            image_copy[a][c].wait_recv()
            work[:, span(c)] += 2.0 * mm(prec[2 + a], images[2 + a, :, span(c)])

        image_copy[2][c].wait_recv()
        work[:, span(c)] += mm(prec[1], images[1, :, span(c)])
        for a in (1, 0):
            given(has_last[a], lambda: quad_last(a))

    norm, curve = collect(0)
    alpha = norm / curve
    out[...] = fields[0] - alpha * images[0]
    work[...] = column * out[...] + (half[...] - alpha * work[...])
    share(1, column_sum(out[...] * out[...]), column_sum(out[...] * work[...]))

    for a in range(2):
        given(has_next[a], lambda: mark_copy[a].wait_send())
        given(has_last[a], lambda: back_copy[a][chunks - 1].wait_send())
        for c in range(chunks):
            given(has_next[a], lambda: field_copy[a][c].wait_send())
            given(has_next[a], lambda: image_copy[a][c].wait_send())
    for c in range(chunks):
        image_copy[2][c].wait_send()

    norm_next, quad = collect(1)
    ratio = norm_next / norm
    alpha_next = norm_next / (quad - ratio * norm_next / alpha)
    out[...] = (alpha + alpha_next * ratio) * fields[0] + alpha_next * out[...]


def shards(sizes, right_side, node_diag, local_coup, block_cols, border_coup, border_send, border_rows):
    size, width = right_side.shape
    nb, nnz, bs, _ = local_coup.shape
    slots = border_coup.shape[1]
    per = slots // 4
    total = sizes[0] * sizes[1] * sizes[2]
    chunks = width // CHUNK
    hbm = pl.BlockSpec(memory_space=pltpu.HBM)
    f32 = jnp.float32
    dma = pltpu.SemaphoreType.DMA
    found = pl.pallas_call(
        functools.partial(kernel, sizes),
        out_shape=jax.ShapeDtypeStruct((size, width), f32),
        in_specs=[hbm] * 7,
        out_specs=pl.BlockSpec(memory_space=pltpu.VMEM),
        scratch_shapes=[
            pltpu.VMEM((4, size, width), f32),
            pltpu.VMEM((4, size, width), f32),
            pltpu.VMEM((2, size, width), f32),
            pltpu.VMEM((2, size, width), f32),
            pltpu.VMEM((nb, nnz, bs, bs), f32),
            pltpu.VMEM((slots, bs, bs), f32),
            pltpu.VMEM((2, per, bs, bs), f32),
            pltpu.VMEM((size, size), f32),
            pltpu.VMEM((size, size), f32),
            pltpu.VMEM((2 * slots, 128), f32),
            pltpu.VMEM((2, 2 * slots, 128), f32),
            pltpu.VMEM((6, size, size), f32),
            pltpu.VMEM((slots, bs, bs), f32),
            pltpu.VMEM((size, width), f32),
            pltpu.VMEM((size, width), f32),
            pltpu.VMEM((2, total, 2, width), f32),
            pltpu.VMEM((1, size), f32),
            pltpu.SMEM((nb, nnz), jnp.int32),
            pltpu.SMEM((1, slots), jnp.int32),
            pltpu.SMEM((1, slots), jnp.int32),
            dma((7,)), dma((3, chunks)), dma((3, chunks)), dma((2,)), dma((2,)), dma((2,)), dma((2,)),
            dma, dma, dma((2, chunks)), dma((2, chunks)), dma((3, chunks)), dma((3, chunks)),
            dma((2,)), dma((2,)),
        ],
        compiler_params=pltpu.CompilerParams(
            collective_id=0, has_side_effects=True
        ),
    )(
        right_side, node_diag.reshape(1, size), local_coup, block_cols, border_coup,
        border_send, border_rows,
    )
    return pl.pallas_call(
        hand_over,
        out_shape=jax.ShapeDtypeStruct((size, width), f32),
        in_specs=[hbm],
        out_specs=hbm,
        scratch_shapes=[dma((PIECES,))],
    )(found)


def solution(mesh):
    in_specs = (
        P(("var", "gx", "gy", "nd"), None),
        P(("var", "gx", "gy", "nd")),
        P(("var", "gx", "gy", "nd"), None, None, None),
        P(("gx", "gy", "nd"), None),
        P(("var", "gx", "gy", "nd"), None, None, None),
        P(("gx", "gy", "nd"), None),
        P(("gx", "gy", "nd"), None),
    )
    out_specs = P(("var", "gx", "gy", "nd"), None)
    sizes = tuple(mesh.shape[axis] for axis in ("gx", "gy", "nd"))
    return jax.shard_map(
        functools.partial(shards, sizes), mesh=mesh, in_specs=in_specs, out_specs=out_specs,
        check_vma=False,
    )
```

```python
import functools

import jax
import jax.numpy as jnp
from jax import lax
from jax.experimental import pallas as pl
from jax.experimental.pallas import tpu as pltpu
from jax.sharding import PartitionSpec as P

LEFT, RIGHT, DOWN, UP = range(4)
CHUNK = 128


def halves(a):
    high = a.astype(jnp.bfloat16)
    return high, (a - high.astype(jnp.float32)).astype(jnp.bfloat16)


def dot(a, b):
    return jnp.dot(a, b, preferred_element_type=jnp.float32)


def mm(a, b):
    a_high, a_low = halves(a)
    b_high, b_low = halves(b)
    width = b.shape[1]
    both = dot(a_high, jnp.concatenate([b_high, b_low], axis=1))
    return both[:, :width] + (both[:, width:] + dot(a_low, b_high))


def column_sum(a):
    return jnp.sum(a, axis=0, keepdims=True)


def kernel(
    sizes,
    rhs, diag_hbm, local, cols_hbm, border, send_hbm, rows_hbm,
    out,
    fields, images, prods_out, prods_in, local_v, border_v, border_in, pair_out, pair_in,
    marks, marks_in, prec, turned, work, half, sums, diag, cols, send, rows,
    load_sem, f_send, f_recv, m_send, m_recv, k_send, k_recv, p_send, p_recv,
    b_send, b_recv, w_send, w_recv, s_send, s_recv,
):
    nx, ny, nn = sizes
    total = nx * ny * nn
    nb, nnz, bs, _ = local_v.shape
    per = border_v.shape[0] // 4
    size, width = out.shape
    chunks = width // CHUNK
    gx, gy, nd = lax.axis_index("gx"), lax.axis_index("gy"), lax.axis_index("nd")
    me = (gx * ny + gy) * nn + nd
    low = gy > 0
    high = gy < ny - 1
    left = {"gx": lax.rem(gx + nx - 1, nx)}
    right = {"gx": lax.rem(gx + 1, nx)}
    below = {"gy": jnp.maximum(gy - 1, 0)}
    above = {"gy": jnp.minimum(gy + 1, ny - 1)}
    partner = {"nd": 1 - nd}
    forward = (right, above)
    backward = (left, below)
    has_next = (None, high)
    has_last = (None, low)
    came = (LEFT, DOWN)
    goes = (RIGHT, UP)

    def given(condition, body):
        if condition is None:
            body()
        else:
            pl.when(condition)(body)

    def part(c):
        return pl.ds(c * CHUNK, CHUNK)

    def span(c):
        return slice(c * CHUNK, (c + 1) * CHUNK)

    def peer(step):
        other = lax.rem(me + step, total)
        return {"gx": other // (ny * nn), "gy": lax.rem(other // nn, ny), "nd": lax.rem(other, nn)}

    def over_peers(body):
        if total <= 16:
            xs = [lax.rem(gx + k, nx) for k in range(nx)]
            ys = [lax.rem(gy + k, ny) for k in range(ny)]
            ns = [lax.rem(nd + k, nn) for k in range(nn)]
            for i in range(nx):
                for j in range(ny):
                    for k in range(nn):
                        if (i, j, k) != (0, 0, 0):
                            body({"gx": xs[i], "gy": ys[j], "nd": ns[k]})
        else:
            lax.fori_loop(1, total, lambda step, _: (body(peer(step)), 0)[1], 0)

    def remote(src, dst, ssem, rsem, where):
        return pltpu.make_async_remote_copy(
            src_ref=src, dst_ref=dst, send_sem=ssem, recv_sem=rsem,
            device_id=where, device_id_type=pl.DeviceIdType.MESH,
        )

    pairs = (
        (send_hbm, send), (rows_hbm, rows), (cols_hbm, cols), (local, local_v),
        (border.at[0], border_v), (rhs, fields.at[0]), (diag_hbm, diag),
    )
    loads = [pltpu.make_async_copy(src, dst, load_sem.at[i]) for i, (src, dst) in enumerate(pairs)]
    for i in (4, 5, 0, 1, 2, 3, 6):
        loads[i].start()

    barrier = pltpu.get_barrier_semaphore()
    over_peers(
        lambda other: pl.semaphore_signal(
            barrier, inc=1, device_id=other, device_id_type=pl.DeviceIdType.MESH
        )
    )
    pl.semaphore_wait(barrier, total - 1)

    mark_copy = [
        remote(marks, marks_in.at[a], k_send.at[a], k_recv.at[a], forward[a]) for a in range(2)
    ]
    border_copy = [
        remote(
            border_v.at[pl.ds(goes[a] * per, per)], border_in.at[a],
            m_send.at[a], m_recv.at[a], forward[a],
        )
        for a in range(2)
    ]
    field_copy = [
        [
            remote(
                fields.at[0, :, part(c)], fields.at[2 + a, :, part(c)],
                f_send.at[a, c], f_recv.at[a, c], forward[a],
            )
            for c in range(chunks)
        ]
        for a in range(2)
    ]
    back_copy = [
        [
            remote(
                prods_out.at[a, :, part(c)], prods_in.at[a, :, part(c)],
                b_send.at[a, c], b_recv.at[a, c], backward[a],
            )
            for c in range(chunks)
        ]
        for a in range(2)
    ]
    image_copy = [
        [
            remote(
                images.at[0, :, part(c)], images.at[slot, :, part(c)],
                w_send.at[i, c], w_recv.at[i, c], where,
            )
            for c in range(chunks)
        ]
        for i, (slot, where) in enumerate(((2, right), (3, above), (1, partner)))
    ]
    field_pair = remote(fields.at[0], fields.at[1], f_send.at[2, 0], f_recv.at[2, 0], partner)
    pair = remote(pair_out, pair_in, p_send, p_recv, partner)

    loads[4].wait()
    for a in range(2):
        given(has_next[a], lambda: border_copy[a].start())
    loads[5].wait()
    field_pair.start()
    loads[0].wait()
    loads[1].wait()
    for m in range(4 * per):
        marks[m : m + 1, :] = jnp.full((1, 128), send[0, m], jnp.int32).astype(jnp.float32)
        at = 4 * per + m
        marks[at : at + 1, :] = jnp.full((1, 128), rows[0, m], jnp.int32).astype(jnp.float32)
    for a in range(2):
        given(has_next[a], lambda: mark_copy[a].start())

    loads[2].wait()
    loads[3].wait()
    for i in range(nb):
        for j in range(nb):
            own = jnp.zeros((bs, bs), jnp.float32)
            far = jnp.zeros((bs, bs), jnp.float32)
            for k in range(nnz):
                block = local_v[i, k]
                col = cols[i, k]
                own = own + jnp.where(col == nd * nb + j, 1.0, 0.0) * block
                far = far + jnp.where(col == (1 - nd) * nb + j, 1.0, 0.0) * block
            prec[0, i * bs : (i + 1) * bs, j * bs : (j + 1) * bs] = own
            pair_out[i * bs : (i + 1) * bs, j * bs : (j + 1) * bs] = far
    pair.start()
    for m in range(4 * per):
        if m // per in came:
            turned[m] = border_v[m].T
    for a in range(2):
        given(has_next[a], lambda: border_copy[a].wait_send())
        given(has_next[a], lambda: field_copy[a][0].start())
    prec[0] = prec[0] + prec[0].T

    loads[6].wait()
    eye = lax.broadcasted_iota(jnp.int32, (size, size), 0) == lax.broadcasted_iota(
        jnp.int32, (size, size), 1
    )
    column = jnp.sum(
        jnp.where(eye, jnp.broadcast_to(diag[...], (size, size)), 0.0), axis=1, keepdims=True
    )
    half[...] = mm(prec[0], fields[0])

    def weights(a, i, j):
        turn, opp = came[a], goes[a]
        for s in range(per):
            m, n = turn * per + s, opp * per + s
            at = 4 * per + n
            yield (
                jnp.where(rows[0, m] == i, 1.0, 0.0)
                * jnp.where(marks_in[a, m : m + 1, :] == float(j), 1.0, 0.0),
                jnp.where(send[0, n] == i, 1.0, 0.0)
                * jnp.where(marks_in[a, at : at + 1, :] == float(j), 1.0, 0.0),
                m,
                s,
            )

    def couple(a):
        mark_copy[a].wait_recv()
        border_copy[a].wait_recv()
        for i in range(nb):
            for j in range(nb):
                block = jnp.zeros((bs, bs), jnp.float32)
                for own, back, m, s in weights(a, i, j):
                    block = block + own * turned[m] + back * border_in[a, s]
                prec[4 + a, j * bs : (j + 1) * bs, i * bs : (i + 1) * bs] = block
        prods_out[a, :, span(0)] = mm(prec[4 + a], fields[0, :, span(0)])
        back_copy[a][0].start()

    def follow(a, c):
        prods_out[a, :, span(c)] = mm(prec[4 + a], fields[0, :, span(c)])
        back_copy[a][c - 1].wait_send()
        back_copy[a][c].start()

    def uncouple(a):
        prec[2 + a] = prec[4 + a].T

    given(has_last[0], lambda: couple(0))
    given(has_last[1], lambda: couple(1))
    pair.wait()
    prec[1] = pair_out[...] + pair_in[...].T
    field_pair.wait()
    half[...] += mm(prec[1], fields[1])
    work[...] = column * fields[0] + half[...]
    for c in range(1, chunks):
        for a in range(2):
            given(has_last[a], lambda: follow(a, c))
            given(has_next[a], lambda: field_copy[a][c].start())
    given(has_last[0], lambda: uncouple(0))
    given(has_last[1], lambda: uncouple(1))

    for c in range(chunks):

        def from_last(a):
            field_copy[a][c].wait_recv()
            term = mm(prec[2 + a], fields[2 + a, :, span(c)])
            work[:, span(c)] += term
            half[:, span(c)] += 2.0 * term

        def from_next(a):
            back_copy[a][c].wait_recv()
            work[:, span(c)] += prods_in[a, :, span(c)]

        for a in (1, 0):
            given(has_last[a], lambda: from_last(a))
            given(has_next[a], lambda: from_next(a))
        images[0, :, span(c)] = work[:, span(c)]
        image_copy[0][c].start()
        given(high, lambda: image_copy[1][c].start())
        image_copy[2][c].start()

    def share(phase, first, second):
        sums[phase, me, 0:1, :] = first
        sums[phase, me, 1:2, :] = second
        over_peers(
            lambda other: remote(
                sums.at[phase, me], sums.at[phase, me], s_send.at[phase], s_recv.at[phase],
                other,
            ).start()
        )

    def collect(phase):
        every = sums.at[phase, pl.ds(0, total - 1)]
        done = remote(every, every, s_send.at[phase], s_recv.at[phase], partner)
        done.wait_send()
        done.wait_recv()
        both = jnp.sum(sums[phase], axis=0)
        return both[0:1, :], both[1:2, :]

    share(0, column_sum(fields[0] * fields[0]), column_sum(fields[0] * images[0]))

    work[...] = mm(prec[0], images[0])
    for c in range(chunks):

        def quad_last(a):
            image_copy[a][c].wait_recv()
            work[:, span(c)] += 2.0 * mm(prec[2 + a], images[2 + a, :, span(c)])

        image_copy[2][c].wait_recv()
        work[:, span(c)] += mm(prec[1], images[1, :, span(c)])
        for a in (1, 0):
            given(has_last[a], lambda: quad_last(a))

    norm, curve = collect(0)
    alpha = norm / curve
    out[...] = fields[0] - alpha * images[0]
    work[...] = column * out[...] + (half[...] - alpha * work[...])
    share(1, column_sum(out[...] * out[...]), column_sum(out[...] * work[...]))

    for a in range(2):
        given(has_next[a], lambda: mark_copy[a].wait_send())
        given(has_last[a], lambda: back_copy[a][chunks - 1].wait_send())
        for c in range(chunks):
            given(has_next[a], lambda: field_copy[a][c].wait_send())
            given(has_next[a], lambda: image_copy[a][c].wait_send())
    for c in range(chunks):
        image_copy[2][c].wait_send()

    norm_next, quad = collect(1)
    ratio = norm_next / norm
    alpha_next = norm_next / (quad - ratio * norm_next / alpha)
    out[...] = (alpha + alpha_next * ratio) * fields[0] + alpha_next * out[...]


def shards(sizes, right_side, node_diag, local_coup, block_cols, border_coup, border_send, border_rows):
    size, width = right_side.shape
    nb, nnz, bs, _ = local_coup.shape
    slots = border_coup.shape[1]
    per = slots // 4
    total = sizes[0] * sizes[1] * sizes[2]
    chunks = width // CHUNK
    hbm = pl.BlockSpec(memory_space=pltpu.HBM)
    f32 = jnp.float32
    dma = pltpu.SemaphoreType.DMA
    return pl.pallas_call(
        functools.partial(kernel, sizes),
        out_shape=jax.ShapeDtypeStruct((size, width), f32),
        in_specs=[hbm] * 7,
        out_specs=pl.BlockSpec(memory_space=pltpu.VMEM),
        scratch_shapes=[
            pltpu.VMEM((4, size, width), f32),
            pltpu.VMEM((4, size, width), f32),
            pltpu.VMEM((2, size, width), f32),
            pltpu.VMEM((2, size, width), f32),
            pltpu.VMEM((nb, nnz, bs, bs), f32),
            pltpu.VMEM((slots, bs, bs), f32),
            pltpu.VMEM((2, per, bs, bs), f32),
            pltpu.VMEM((size, size), f32),
            pltpu.VMEM((size, size), f32),
            pltpu.VMEM((2 * slots, 128), f32),
            pltpu.VMEM((2, 2 * slots, 128), f32),
            pltpu.VMEM((6, size, size), f32),
            pltpu.VMEM((slots, bs, bs), f32),
            pltpu.VMEM((size, width), f32),
            pltpu.VMEM((size, width), f32),
            pltpu.VMEM((2, total, 2, width), f32),
            pltpu.VMEM((1, size), f32),
            pltpu.SMEM((nb, nnz), jnp.int32),
            pltpu.SMEM((1, slots), jnp.int32),
            pltpu.SMEM((1, slots), jnp.int32),
            dma((7,)), dma((3, chunks)), dma((3, chunks)), dma((2,)), dma((2,)), dma((2,)), dma((2,)),
            dma, dma, dma((2, chunks)), dma((2, chunks)), dma((3, chunks)), dma((3, chunks)),
            dma((2,)), dma((2,)),
        ],
        compiler_params=pltpu.CompilerParams(
            collective_id=0, has_side_effects=True
        ),
    )(
        right_side, node_diag.reshape(1, size), local_coup, block_cols, border_coup,
        border_send, border_rows,
    )


def solution(mesh):
    in_specs = (
        P(("var", "gx", "gy", "nd"), None),
        P(("var", "gx", "gy", "nd")),
        P(("var", "gx", "gy", "nd"), None, None, None),
        P(("gx", "gy", "nd"), None),
        P(("var", "gx", "gy", "nd"), None, None, None),
        P(("gx", "gy", "nd"), None),
        P(("gx", "gy", "nd"), None),
    )
    out_specs = P(("var", "gx", "gy", "nd"), None)
    sizes = tuple(mesh.shape[axis] for axis in ("gx", "gy", "nd"))
    return jax.shard_map(
        functools.partial(shards, sizes), mesh=mesh, in_specs=in_specs, out_specs=out_specs,
        check_vma=False,
    )
```

```python
import functools

import jax
import jax.numpy as jnp
from jax import lax
from jax.experimental import pallas as pl
from jax.experimental.pallas import tpu as pltpu
from jax.sharding import PartitionSpec as P

LEFT, RIGHT, DOWN, UP = range(4)
CHUNK = 128


def halves(a):
    high = a.astype(jnp.bfloat16)
    return high, (a - high.astype(jnp.float32)).astype(jnp.bfloat16)


def dot(a, b):
    return jnp.dot(a, b, preferred_element_type=jnp.float32)


def mm(a, b):
    a_high, a_low = halves(a)
    b_high, b_low = halves(b)
    width = b.shape[1]
    both = dot(a_high, jnp.concatenate([b_high, b_low], axis=1))
    return both[:, :width] + (both[:, width:] + dot(a_low, b_high))


def column_sum(a):
    return jnp.sum(a, axis=0, keepdims=True)


def kernel(
    sizes,
    rhs, diag_hbm, local, cols_hbm, border, send_hbm, rows_hbm,
    out,
    fields, images, prods_out, prods_in, local_v, border_v, border_in, pair_out, pair_in,
    marks, marks_in, prec, turned, work, half, sums, diag, cols, send, rows,
    load_sem, f_send, f_recv, m_send, m_recv, k_send, k_recv, p_send, p_recv,
    b_send, b_recv, w_send, w_recv, s_send, s_recv,
):
    nx, ny, nn = sizes
    total = nx * ny * nn
    nb, nnz, bs, _ = local_v.shape
    per = border_v.shape[0] // 4
    size, width = out.shape
    chunks = width // CHUNK
    gx, gy, nd = lax.axis_index("gx"), lax.axis_index("gy"), lax.axis_index("nd")
    me = (gx * ny + gy) * nn + nd
    low = gy > 0
    high = gy < ny - 1
    left = {"gx": lax.rem(gx + nx - 1, nx)}
    right = {"gx": lax.rem(gx + 1, nx)}
    below = {"gy": jnp.maximum(gy - 1, 0)}
    above = {"gy": jnp.minimum(gy + 1, ny - 1)}
    partner = {"nd": 1 - nd}
    forward = (right, above)
    backward = (left, below)
    has_next = (None, high)
    has_last = (None, low)
    came = (LEFT, DOWN)
    goes = (RIGHT, UP)

    def given(condition, body):
        if condition is None:
            body()
        else:
            pl.when(condition)(body)

    def part(c):
        return pl.ds(c * CHUNK, CHUNK)

    def span(c):
        return slice(c * CHUNK, (c + 1) * CHUNK)

    def peer(step):
        other = lax.rem(me + step, total)
        return {"gx": other // (ny * nn), "gy": lax.rem(other // nn, ny), "nd": lax.rem(other, nn)}

    def over_peers(body):
        if total <= 16:
            xs = [lax.rem(gx + k, nx) for k in range(nx)]
            ys = [lax.rem(gy + k, ny) for k in range(ny)]
            ns = [lax.rem(nd + k, nn) for k in range(nn)]
            for i in range(nx):
                for j in range(ny):
                    for k in range(nn):
                        if (i, j, k) != (0, 0, 0):
                            body({"gx": xs[i], "gy": ys[j], "nd": ns[k]})
        else:
            lax.fori_loop(1, total, lambda step, _: (body(peer(step)), 0)[1], 0)

    def remote(src, dst, ssem, rsem, where):
        return pltpu.make_async_remote_copy(
            src_ref=src, dst_ref=dst, send_sem=ssem, recv_sem=rsem,
            device_id=where, device_id_type=pl.DeviceIdType.MESH,
        )

    pairs = (
        (send_hbm, send), (rows_hbm, rows), (cols_hbm, cols), (local, local_v),
        (border.at[0], border_v), (rhs, fields.at[0]), (diag_hbm, diag),
    )
    loads = [pltpu.make_async_copy(src, dst, load_sem.at[i]) for i, (src, dst) in enumerate(pairs)]
    for i in (4, 5, 0, 1, 2, 3, 6):
        loads[i].start()

    barrier = pltpu.get_barrier_semaphore()
    over_peers(
        lambda other: pl.semaphore_signal(
            barrier, inc=1, device_id=other, device_id_type=pl.DeviceIdType.MESH
        )
    )
    pl.semaphore_wait(barrier, total - 1)

    mark_copy = [
        remote(marks, marks_in.at[a], k_send.at[a], k_recv.at[a], forward[a]) for a in range(2)
    ]
    border_copy = [
        remote(
            border_v.at[pl.ds(goes[a] * per, per)], border_in.at[a],
            m_send.at[a], m_recv.at[a], forward[a],
        )
        for a in range(2)
    ]
    field_copy = [
        [
            remote(
                fields.at[0, :, part(c)], fields.at[2 + a, :, part(c)],
                f_send.at[a, c], f_recv.at[a, c], forward[a],
            )
            for c in range(chunks)
        ]
        for a in range(2)
    ]
    back_copy = [
        [
            remote(
                prods_out.at[a, :, part(c)], prods_in.at[a, :, part(c)],
                b_send.at[a, c], b_recv.at[a, c], backward[a],
            )
            for c in range(chunks)
        ]
        for a in range(2)
    ]
    image_copy = [
        [
            remote(
                images.at[0, :, part(c)], images.at[slot, :, part(c)],
                w_send.at[i, c], w_recv.at[i, c], where,
            )
            for c in range(chunks)
        ]
        for i, (slot, where) in enumerate(((2, right), (3, above), (1, partner)))
    ]
    field_pair = remote(fields.at[0], fields.at[1], f_send.at[2, 0], f_recv.at[2, 0], partner)
    pair = remote(pair_out, pair_in, p_send, p_recv, partner)

    loads[4].wait()
    for a in range(2):
        given(has_next[a], lambda: border_copy[a].start())
    loads[5].wait()
    field_pair.start()
    loads[0].wait()
    loads[1].wait()
    for m in range(4 * per):
        marks[m : m + 1, :] = jnp.full((1, 128), send[0, m], jnp.int32).astype(jnp.float32)
        at = 4 * per + m
        marks[at : at + 1, :] = jnp.full((1, 128), rows[0, m], jnp.int32).astype(jnp.float32)
    for a in range(2):
        given(has_next[a], lambda: mark_copy[a].start())

    loads[2].wait()
    loads[3].wait()
    for i in range(nb):
        for j in range(nb):
            own = jnp.zeros((bs, bs), jnp.float32)
            far = jnp.zeros((bs, bs), jnp.float32)
            for k in range(nnz):
                block = local_v[i, k]
                col = cols[i, k]
                own = own + jnp.where(col == nd * nb + j, 1.0, 0.0) * block
                far = far + jnp.where(col == (1 - nd) * nb + j, 1.0, 0.0) * block
            prec[0, i * bs : (i + 1) * bs, j * bs : (j + 1) * bs] = own
            pair_out[i * bs : (i + 1) * bs, j * bs : (j + 1) * bs] = far
    pair.start()
    for m in range(4 * per):
        if m // per in came:
            turned[m] = border_v[m].T
    for a in range(2):
        given(has_next[a], lambda: border_copy[a].wait_send())
        given(has_next[a], lambda: field_copy[a][0].start())
    prec[0] = prec[0] + prec[0].T

    loads[6].wait()
    eye = lax.broadcasted_iota(jnp.int32, (size, size), 0) == lax.broadcasted_iota(
        jnp.int32, (size, size), 1
    )
    column = jnp.sum(
        jnp.where(eye, jnp.broadcast_to(diag[...], (size, size)), 0.0), axis=1, keepdims=True
    )
    half[...] = mm(prec[0], fields[0])

    def weights(a, i, j):
        turn, opp = came[a], goes[a]
        for s in range(per):
            m, n = turn * per + s, opp * per + s
            at = 4 * per + n
            yield (
                jnp.where(rows[0, m] == i, 1.0, 0.0)
                * jnp.where(marks_in[a, m : m + 1, :] == float(j), 1.0, 0.0),
                jnp.where(send[0, n] == i, 1.0, 0.0)
                * jnp.where(marks_in[a, at : at + 1, :] == float(j), 1.0, 0.0),
                m,
                s,
            )

    def couple(a):
        mark_copy[a].wait_recv()
        border_copy[a].wait_recv()
        for i in range(nb):
            for j in range(nb):
                block = jnp.zeros((bs, bs), jnp.float32)
                for own, back, m, s in weights(a, i, j):
                    block = block + own * turned[m] + back * border_in[a, s]
                prec[4 + a, j * bs : (j + 1) * bs, i * bs : (i + 1) * bs] = block
        prods_out[a, :, span(0)] = mm(prec[4 + a], fields[0, :, span(0)])
        back_copy[a][0].start()

    def follow(a, c):
        prods_out[a, :, span(c)] = mm(prec[4 + a], fields[0, :, span(c)])
        back_copy[a][c - 1].wait_send()
        back_copy[a][c].start()

    def uncouple(a):
        prec[2 + a] = prec[4 + a].T

    given(has_last[0], lambda: couple(0))
    given(has_last[1], lambda: couple(1))
    pair.wait()
    prec[1] = pair_out[...] + pair_in[...].T
    field_pair.wait()
    half[...] += mm(prec[1], fields[1])
    work[...] = column * fields[0] + half[...]
    for c in range(1, chunks):
        for a in range(2):
            given(has_last[a], lambda: follow(a, c))
            given(has_next[a], lambda: field_copy[a][c].start())
    given(has_last[0], lambda: uncouple(0))
    given(has_last[1], lambda: uncouple(1))

    def share(phase, first, second):
        sums[phase, me, 0:1, :] = first
        sums[phase, me, 1:2, :] = second
        over_peers(
            lambda other: remote(
                sums.at[phase, me], sums.at[phase, me], s_send.at[phase], s_recv.at[phase],
                other,
            ).start()
        )

    norm_here = column_sum(fields[0] * fields[0])
    for c in range(chunks):

        def from_last(a):
            field_copy[a][c].wait_recv()
            term = mm(prec[2 + a], fields[2 + a, :, span(c)])
            work[:, span(c)] += term
            half[:, span(c)] += 2.0 * term

        def from_next(a):
            back_copy[a][c].wait_recv()
            work[:, span(c)] += prods_in[a, :, span(c)]

        for a in (1, 0):
            given(has_last[a], lambda: from_last(a))
            given(has_next[a], lambda: from_next(a))
        images[0, :, span(c)] = work[:, span(c)]
        if c == chunks - 1:
            share(0, norm_here, column_sum(fields[0] * images[0]))
        image_copy[0][c].start()
        given(high, lambda: image_copy[1][c].start())
        image_copy[2][c].start()

    def collect(phase):
        every = sums.at[phase, pl.ds(0, total - 1)]
        done = remote(every, every, s_send.at[phase], s_recv.at[phase], partner)
        done.wait_send()
        done.wait_recv()
        both = jnp.sum(sums[phase], axis=0)
        return both[0:1, :], both[1:2, :]


    work[...] = mm(prec[0], images[0])
    for c in range(chunks):

        def quad_last(a):
            image_copy[a][c].wait_recv()
            work[:, span(c)] += 2.0 * mm(prec[2 + a], images[2 + a, :, span(c)])

        image_copy[2][c].wait_recv()
        work[:, span(c)] += mm(prec[1], images[1, :, span(c)])
        for a in (1, 0):
            given(has_last[a], lambda: quad_last(a))

    norm, curve = collect(0)
    alpha = norm / curve
    out[...] = fields[0] - alpha * images[0]
    work[...] = column * out[...] + (half[...] - alpha * work[...])
    share(1, column_sum(out[...] * out[...]), column_sum(out[...] * work[...]))

    for a in range(2):
        given(has_next[a], lambda: mark_copy[a].wait_send())
        given(has_last[a], lambda: back_copy[a][chunks - 1].wait_send())
        for c in range(chunks):
            given(has_next[a], lambda: field_copy[a][c].wait_send())
            given(has_next[a], lambda: image_copy[a][c].wait_send())
    for c in range(chunks):
        image_copy[2][c].wait_send()

    norm_next, quad = collect(1)
    ratio = norm_next / norm
    alpha_next = norm_next / (quad - ratio * norm_next / alpha)
    out[...] = (alpha + alpha_next * ratio) * fields[0] + alpha_next * out[...]


def shards(sizes, right_side, node_diag, local_coup, block_cols, border_coup, border_send, border_rows):
    size, width = right_side.shape
    nb, nnz, bs, _ = local_coup.shape
    slots = border_coup.shape[1]
    per = slots // 4
    total = sizes[0] * sizes[1] * sizes[2]
    chunks = width // CHUNK
    hbm = pl.BlockSpec(memory_space=pltpu.HBM)
    f32 = jnp.float32
    dma = pltpu.SemaphoreType.DMA
    return pl.pallas_call(
        functools.partial(kernel, sizes),
        out_shape=jax.ShapeDtypeStruct((size, width), f32),
        in_specs=[hbm] * 7,
        out_specs=pl.BlockSpec(memory_space=pltpu.VMEM),
        scratch_shapes=[
            pltpu.VMEM((4, size, width), f32),
            pltpu.VMEM((4, size, width), f32),
            pltpu.VMEM((2, size, width), f32),
            pltpu.VMEM((2, size, width), f32),
            pltpu.VMEM((nb, nnz, bs, bs), f32),
            pltpu.VMEM((slots, bs, bs), f32),
            pltpu.VMEM((2, per, bs, bs), f32),
            pltpu.VMEM((size, size), f32),
            pltpu.VMEM((size, size), f32),
            pltpu.VMEM((2 * slots, 128), f32),
            pltpu.VMEM((2, 2 * slots, 128), f32),
            pltpu.VMEM((6, size, size), f32),
            pltpu.VMEM((slots, bs, bs), f32),
            pltpu.VMEM((size, width), f32),
            pltpu.VMEM((size, width), f32),
            pltpu.VMEM((2, total, 2, width), f32),
            pltpu.VMEM((1, size), f32),
            pltpu.SMEM((nb, nnz), jnp.int32),
            pltpu.SMEM((1, slots), jnp.int32),
            pltpu.SMEM((1, slots), jnp.int32),
            dma((7,)), dma((3, chunks)), dma((3, chunks)), dma((2,)), dma((2,)), dma((2,)), dma((2,)),
            dma, dma, dma((2, chunks)), dma((2, chunks)), dma((3, chunks)), dma((3, chunks)),
            dma((2,)), dma((2,)),
        ],
        compiler_params=pltpu.CompilerParams(
            collective_id=0, has_side_effects=True
        ),
    )(
        right_side, node_diag.reshape(1, size), local_coup, block_cols, border_coup,
        border_send, border_rows,
    )


def solution(mesh):
    in_specs = (
        P(("var", "gx", "gy", "nd"), None),
        P(("var", "gx", "gy", "nd")),
        P(("var", "gx", "gy", "nd"), None, None, None),
        P(("gx", "gy", "nd"), None),
        P(("var", "gx", "gy", "nd"), None, None, None),
        P(("gx", "gy", "nd"), None),
        P(("gx", "gy", "nd"), None),
    )
    out_specs = P(("var", "gx", "gy", "nd"), None)
    sizes = tuple(mesh.shape[axis] for axis in ("gx", "gy", "nd"))
    return jax.shard_map(
        functools.partial(shards, sizes), mesh=mesh, in_specs=in_specs, out_specs=out_specs,
        check_vma=False,
    )
```
